128 devices in a mesh: role: 2 (over core), rows: 16 (over z, y), heads: 4 (over x).
Axes of the slice: x: 4, y: 4, z: 4, core: 2. Of those that a mesh axis runs over, the one named last changes fastest.
Arguments:
- queries: bfloat16 [512, 2, 4, 1024], P('rows', 'role', 'heads'), may hold values from -9 to 9
- k_cache: bfloat16 [512, 4, 512, 128], P('rows', 'heads'), may hold values from -6 to 6
- value_cache: bfloat16 [512, 4, 512, 128], P('rows', 'heads'), may hold values from -6 to 6
- new_token_key: bfloat16 [512, 4, 128], P('rows', 'heads'), may hold values from -6 to 6
- new_token_value: bfloat16 [512, 4, 128], P('rows', 'heads'), may hold values from -6 to 6
- lengths: int32 [512], P('rows'), may hold values from 2 to 512, as said below
- output_weight: bfloat16 [2, 4, 1024, 4096], P('role', 'heads'), may hold values from -0.5 to 0.5
- residual: bfloat16 [512, 4096], P('rows'), may hold values from -60 to 60
- norm_gain: float32 [4096], replicated, may hold values from 0.5 to 2
- routes: int32 [512, 8], P('rows'), may hold values from 0 to 63, all different within a row; in each aligned block of 32 rows (0 to 31, 32 to 63, ...) at most 8 rows name the same one
- route_scores: float32 [512, 8], P('rows'), may hold values from 0.05 to 1
- w_gate: bfloat16 [64, 4096, 1024], P(('role', 'rows'), None, 'heads'), may hold values from -0.09375 to 0.09375
- w_up: bfloat16 [64, 4096, 1024], P(('role', 'rows'), None, 'heads'), may hold values from -0.09375 to 0.09375
- w_down: bfloat16 [64, 1024, 4096], P(('role', 'rows'), 'heads'), may hold values from -0.1875 to 0.1875
Outputs:
- final: bfloat16 [512, 4096], P('rows', ('role', 'heads'))
The draws below stay inside these ranges and needn't reach their ends.
Inputs may be any that keep to these rules, and one draw needn't show every extreme that they name: `lengths`: at least one row holds 512 cached positions. `routes`: each row names 8 different experts; the 32 rows of one index of rows name no expert more than 8 times, a bound that some block reaches.
All inputs are finite; a program needn't handle non-finite values.
Results may differ from the reference program's by a relative error of at most 0.015.
Values may be sent and summed in bfloat16 or wider, within the bound.
No kernel may reach another device: no remote copies, remote signals or barrier semaphores. Data moves between devices by JAX's collectives and lax.ppermute only.
A program may use at most 128 MiB of HBM per device.

```python
import math
import jax
import jax.numpy as jnp
import numpy as np
from jax import lax

MODEL_WIDTH = 4096
QUERY_HEADS = 64
KEY_VALUE_HEADS = 4
HEAD_DIMENSION = 128
QUERIES_PER_HEAD = 8
ROW_DEV = 32
ROLLOUT_ROWS = 512
CACHE_POSITIONS = 512
TOP = 8
EXPERTS = 64
FFE = 1024
CAP = 8
N_ROLE = 2
N_HEADS = 4


def shared_query(key):
    query_start = jax.random.normal(jax.random.fold_in(key, 101), (ROLLOUT_ROWS, N_ROLE, KEY_VALUE_HEADS, QUERIES_PER_HEAD * HEAD_DIMENSION), jnp.float32)
    query_start = jnp.clip(query_start, -6.0, 6.0)
    return query_start


def draw_queries(key, part):
    query_start = shared_query(key)
    value_rows = query_start
    return value_rows.astype(jnp.bfloat16)


def draw_k_cache(key, part):
    key = jax.random.fold_in(key, 2)
    value_rows = jnp.clip(jax.random.normal(key, (ROLLOUT_ROWS, KEY_VALUE_HEADS, CACHE_POSITIONS, HEAD_DIMENSION), jnp.float32), -6.0, 6.0)
    return value_rows.astype(jnp.bfloat16)


def draw_lengths(key, part):
    key = jax.random.fold_in(key, 3)
    tries = jax.random.randint(key, (3, ROLLOUT_ROWS), 2, CACHE_POSITIONS + 1)
    shortest = jnp.min(tries, axis=0)
    pick = jax.random.randint(jax.random.fold_in(key, 7), (), 0, ROLLOUT_ROWS)
    return jnp.where(jnp.arange(ROLLOUT_ROWS) == pick, CACHE_POSITIONS, shortest).astype(jnp.int32)


def draw_residual(key, part):
    key = jax.random.fold_in(key, 4)
    column = jnp.arange(MODEL_WIDTH, dtype=jnp.float32) / MODEL_WIDTH - 0.5
    row_scale = jnp.exp(jax.random.uniform(jax.random.fold_in(key, 11), (ROLLOUT_ROWS, 1), jnp.float32, math.log(0.3), math.log(3.0)))
    col_scale = jnp.exp(jax.random.uniform(jax.random.fold_in(key, 12), (MODEL_WIDTH,), jnp.float32, -1.15, 1.15))
    base = jnp.clip(jax.random.normal(jax.random.fold_in(key, 13), (ROLLOUT_ROWS, MODEL_WIDTH), jnp.float32), -5.0, 5.0)
    rising = jnp.exp(column * math.log(3.0))
    return (base * row_scale * col_scale * rising).astype(jnp.bfloat16)


def levels(stream_key, extent, cuts, smallest, largest):
    level, own = 1.0, jax.random.fold_in(stream_key, 6)
    for dim, shards_of in cuts:
        heights = jnp.exp(jax.random.uniform(jax.random.fold_in(own, dim), (shards_of,), jnp.float32, smallest / len(cuts), largest / len(cuts)))
        level = level * jnp.repeat(heights, extent[dim] // shards_of).reshape([-1 if axis == dim else 1 for axis in range(len(extent))])
    return level


def deal_out(key, own, number, rows, count, top, reach, skew):
    sequence = jax.random.permutation(key, count)
    crowded, ordinary = load_shares(count, rows * top, reach, skew, True), load_shares(count, rows * top, reach, skew, False)
    places = jnp.arange(count)

    def named(sizes, rotation):
        used = int((sizes > 0).sum())
        fixed = max(1, used // 4)
        moved = fixed + (places - fixed + rotation * (used - fixed)) % max(1, count - fixed)
        return jnp.zeros((count,), jnp.int32).at[sequence[jnp.where(places < fixed, places, moved)]].set(jnp.asarray(sizes, jnp.int32))

    sizes = jnp.where(number % 4 == 0, named(crowded, number // 4), named(ordinary, number - number // 4 - 1))
    mixed = jax.random.permutation(jax.random.fold_in(own, 3), count)
    source_of, taker = mixed[0:count // 2 * 2:2], mixed[1:count // 2 * 2:2]
    slack = jnp.minimum(sizes[source_of] - 1, reach - sizes[taker]) // 2
    slack = jnp.where((source_of == sequence[0]) | (taker == sequence[0]) | (sizes[taker] == 0), 0, jnp.maximum(slack, 0))
    moved = jax.random.randint(jax.random.fold_in(own, 4), (count // 2,), 0, 1 << 20) % (slack + 1)
    sizes = sizes.at[source_of].add(-moved).at[taker].add(moved)
    items = jnp.searchsorted(jnp.cumsum(sizes), jnp.arange(rows * top), side="right").astype(jnp.int32)
    grid = items.reshape(top, rows).T
    grid = grid[jax.random.permutation(jax.random.fold_in(own, 1), rows)]
    rotation = jax.random.randint(jax.random.fold_in(own, 2), (rows, 1), 0, top)
    return jnp.take_along_axis(grid, (jnp.arange(top)[None, :] + rotation) % top, axis=1)


def load_shares(number_of, total, bound, skew, full):
    weights = [(1 << 20) // math.isqrt(rank ** skew) + 1 for rank in range(1, number_of + 1)]
    largest = bound if full else min(bound, max(-(-total // number_of), total * weights[0] // sum(weights)))
    least = 1 if total - largest >= number_of - 1 else 0
    counts, spare = [largest] + [least] * (number_of - 1), total - largest - least * (number_of - 1)
    while spare > 0:
        candidates = [i for i in range(1, number_of) if counts[i] < largest] or [i for i in range(1, number_of) if counts[i] < bound]
        pool, left = sum([weights[i] for i in candidates]), spare
        for i in candidates:
            more = min(bound - counts[i], max(1, left * weights[i] // pool), spare)
            counts[i] = counts[i] + more
            spare = spare - more
    return np.array(counts)


def gaussian(key, dims, spread, limit, split=(), kind=jnp.bfloat16):
    gain = levels(key, dims, split, -0.22, 0.18) if split else 1.0
    values = jax.random.normal(key, dims, jnp.float32) * spread * gain
    return jnp.minimum(jnp.maximum(values, -limit), limit).astype(kind)


def setup_inputs(seed: int = 0) -> dict:
    keys = jax.random.split(jax.random.key(seed), 15)
    queries = draw_queries(jax.random.fold_in(keys[14], 71), 0)
    k_cache = draw_k_cache(jax.random.fold_in(keys[14], 71), 0)
    value_cache = gaussian(keys[2], (ROLLOUT_ROWS, KEY_VALUE_HEADS, CACHE_POSITIONS, HEAD_DIMENSION), 1.0, 6.0, ((0, 16), (1, 4)))
    new_token_key = gaussian(keys[3], (ROLLOUT_ROWS, KEY_VALUE_HEADS, HEAD_DIMENSION), 1.0, 6.0, ((0, 16), (1, 4)))
    new_token_value = gaussian(keys[4], (ROLLOUT_ROWS, KEY_VALUE_HEADS, HEAD_DIMENSION), 1.0, 6.0, ((0, 16), (1, 4)))
    lengths = draw_lengths(jax.random.fold_in(keys[14], 71), 0)
    output_weight = gaussian(keys[6], (N_ROLE, KEY_VALUE_HEADS, QUERIES_PER_HEAD * HEAD_DIMENSION, MODEL_WIDTH), (QUERY_HEADS * HEAD_DIMENSION // 64) ** -0.5, 0.5, ((0, 2), (1, 4)))
    residual = draw_residual(jax.random.fold_in(keys[14], 71), 0)
    norm_gain = jnp.clip(jax.random.uniform(keys[8], (MODEL_WIDTH,), jnp.float32, 0.5, 2.0), 0.5, 2.0)
    routes_keys = jax.random.split(jax.random.fold_in(keys[9], 1), ROLLOUT_ROWS // ROW_DEV)
    routes_turns = jax.random.permutation(jax.random.fold_in(keys[9], 3), ROLLOUT_ROWS // ROW_DEV)
    routes = jax.vmap(lambda own, number: deal_out(jax.random.fold_in(keys[9], 2), own, number, ROW_DEV, EXPERTS, TOP, CAP, 2))(routes_keys, routes_turns).reshape((ROLLOUT_ROWS, TOP))
    route_scores = jnp.clip(jnp.exp(math.log(1.0) - 2.9957323 * jax.random.uniform(keys[10], (ROLLOUT_ROWS, TOP), jnp.float32) ** levels(keys[10], (ROLLOUT_ROWS, TOP), ((0, 16),), -0.2, 0.2)), 0.05, 1.0)
    w_gate = gaussian(keys[11], (EXPERTS, MODEL_WIDTH, FFE), MODEL_WIDTH ** -0.5, 0.09375, ((0, 32), (2, 4)))
    w_up = gaussian(keys[12], (EXPERTS, MODEL_WIDTH, FFE), MODEL_WIDTH ** -0.5, 0.09375, ((0, 32), (2, 4)))
    w_down = gaussian(keys[13], (EXPERTS, FFE, MODEL_WIDTH), FFE ** -0.5, 0.1875, ((0, 32), (1, 4)))
    return dict(queries=queries, k_cache=k_cache, value_cache=value_cache, new_token_key=new_token_key, new_token_value=new_token_value, lengths=lengths, output_weight=output_weight, residual=residual, norm_gain=norm_gain, routes=routes, route_scores=route_scores, w_gate=w_gate, w_up=w_up, w_down=w_down)


def reference(queries, k_cache, value_cache, new_token_key, new_token_value, lengths, output_weight, residual, norm_gain, routes, route_scores, w_gate, w_up, w_down):
    root = math.sqrt(HEAD_DIMENSION)
    query_vectors = queries.astype(jnp.float32).reshape(ROLLOUT_ROWS, N_ROLE, KEY_VALUE_HEADS, QUERIES_PER_HEAD, HEAD_DIMENSION)
    scores = jnp.einsum('rsgqd,rgld->rsgql', query_vectors, k_cache.astype(jnp.float32)) / root
    fresh = jnp.einsum('rsgqd,rgd->rsgq', query_vectors, new_token_key.astype(jnp.float32)) / root
    valid = jnp.arange(CACHE_POSITIONS, dtype=jnp.int32)[None, :] < lengths[:, None]
    scores = jnp.where(valid[:, None, None, None, :], scores, -jnp.inf)
    top = jnp.maximum(lax.optimization_barrier(jnp.max(scores, axis=-1)), fresh)
    expo = jnp.exp(scores - top[..., None])
    expo_new = jnp.exp(fresh - top)
    denom = lax.optimization_barrier(jnp.sum(expo, axis=-1)) + expo_new
    probs = (expo / denom[..., None]).astype(jnp.bfloat16)
    probs_new = (expo_new / denom).astype(jnp.bfloat16)
    attention_result = jnp.einsum('rsgql,rgld->rsgqd', probs.astype(jnp.float32), value_cache.astype(jnp.float32))
    attention_result = attention_result + probs_new.astype(jnp.float32)[..., None] * new_token_value.astype(jnp.float32)[:, None, :, None, :]
    attention_result = attention_result.astype(jnp.bfloat16).reshape(ROLLOUT_ROWS, N_ROLE, KEY_VALUE_HEADS, QUERIES_PER_HEAD * HEAD_DIMENSION)
    attended = jnp.einsum('rsgk,sgkd->rd', attention_result.astype(jnp.float32), output_weight.astype(jnp.float32))
    hidden = residual.astype(jnp.float32) + attended
    meansq = lax.optimization_barrier(jnp.mean(hidden * hidden, axis=1, keepdims=True))
    normed = (hidden * lax.rsqrt(meansq + 1e-06) * norm_gain).astype(jnp.bfloat16)
    weights = route_scores / lax.optimization_barrier(jnp.sum(route_scores, axis=1, keepdims=True))
    chosen = routes[:, :, None] == jnp.arange(EXPERTS, dtype=jnp.int32)[None, None, :]
    coef = lax.optimization_barrier(jnp.sum(jnp.where(chosen, weights[:, :, None], jnp.float32(0.0)), axis=1))
    quarter = FFE // N_HEADS

    def one_expert(total, items):
        gate_w, up_w, down_w, column = items
        gate = jnp.dot(normed, gate_w, preferred_element_type=jnp.float32)
        upper = jnp.dot(normed, up_w, preferred_element_type=jnp.float32)
        act = (jax.nn.silu(gate) * upper).astype(jnp.bfloat16)
        parts = jnp.einsum('rqf,qfd->rqd', act.reshape(ROLLOUT_ROWS, N_HEADS, quarter).astype(jnp.float32), down_w.reshape(N_HEADS, quarter, MODEL_WIDTH).astype(jnp.float32))
        summed = lax.optimization_barrier(jnp.sum(parts.astype(jnp.bfloat16).astype(jnp.float32), axis=1))
        return (total + column[:, None] * summed, None)
    moe, unused = lax.scan(one_expert, jnp.zeros((ROLLOUT_ROWS, MODEL_WIDTH), jnp.float32), (w_gate, w_up, w_down, coef.T))
    return (hidden + moe).astype(jnp.bfloat16)
```

```python
import math

import jax
import jax.numpy as jnp
from jax import lax
from jax.sharding import PartitionSpec as P

BF = jnp.bfloat16
F32 = jnp.float32
EPS = 1e-06


def attention(queries, k_cache, value_cache, new_token_key, new_token_value, lengths):
    rows_here = queries.shape[0]
    head_size = k_cache.shape[3]
    cache_len = k_cache.shape[2]
    per_group = queries.shape[3] // head_size
    root = math.sqrt(head_size)
    query_vectors = queries[:, 0, 0].reshape(rows_here, per_group, head_size)
    scores = jnp.einsum("rqd,rld->rql", query_vectors, k_cache[:, 0], preferred_element_type=F32)
    scores = scores / root
    fresh = jnp.einsum("rqd,rd->rq", query_vectors, new_token_key[:, 0], preferred_element_type=F32)
    fresh = fresh / root
    valid = lax.broadcasted_iota(jnp.int32, (rows_here, cache_len), 1) < lengths[:, None]
    scores = jnp.where(valid[:, None, :], scores, -jnp.inf)
    top = jnp.maximum(jnp.max(scores, axis=-1), fresh)
    expo = jnp.exp(scores - top[..., None])
    expo_new = jnp.exp(fresh - top)
    denom = jnp.sum(expo, axis=-1) + expo_new
    probs = (expo / denom[..., None]).astype(BF)
    probs_new = (expo_new / denom).astype(BF)
    result = jnp.einsum("rql,rld->rqd", probs, value_cache[:, 0], preferred_element_type=F32)
    result = result + probs_new.astype(F32)[..., None] * new_token_value[:, 0].astype(F32)[:, None]
    return result.astype(BF).reshape(rows_here, per_group * head_size)


def per_device(
    queries,
    k_cache,
    value_cache,
    new_token_key,
    new_token_value,
    lengths,
    output_weight,
    residual,
    norm_gain,
    routes,
    route_scores,
    w_gate,
    w_up,
    w_down,
):
    rows_here = queries.shape[0]
    width = residual.shape[1]
    roles = lax.axis_size("role")
    heads_count = lax.axis_size("heads")
    shards = lax.axis_size("rows")
    half = width // roles
    piece = half // heads_count
    per_dev, _, quarter = w_gate.shape
    experts = per_dev * shards * roles
    capacity = 8
    role = lax.axis_index("role")
    head = lax.axis_index("heads")
    swap = [(i, roles - 1 - i) for i in range(roles)]

    def shift(x, step):
        return lax.ppermute(
            x, "heads", [(i, (i + step) % heads_count) for i in range(heads_count)]
        )

    down = w_down.reshape(per_dev, quarter, roles, heads_count, piece)
    downs = []
    for step in range(heads_count):
        part = lax.dynamic_slice_in_dim(down, (head + step) % heads_count, 1, 3)
        part = part.reshape(per_dev, quarter, roles * piece)
        downs.append(part if step == 0 else shift(part, step))

    attended = attention(
        queries, k_cache, value_cache, new_token_key, new_token_value, lengths
    )
    partial = jnp.dot(attended, output_weight[0, 0], preferred_element_type=F32)
    low, high = partial[:, :half], partial[:, half:]
    first = role == 0
    theirs = jnp.where(first, high, low).astype(BF)
    mine = jnp.where(first, low, high)
    chip = (mine + lax.ppermute(theirs, "role", swap).astype(F32)).astype(BF)
    total = chip.astype(F32)
    for step in range(1, heads_count):
        total = total + shift(chip, step).astype(F32)
    resid = jnp.where(first, residual[:, :half], residual[:, half:]).astype(F32)
    gain = jnp.where(first, norm_gain[:half], norm_gain[half:])
    hidden = resid + total
    scaled = (hidden * gain).astype(BF)

    named = routes[:, :, None] == jnp.arange(experts, dtype=jnp.int32)
    chosen = jnp.any(named, axis=1)
    shares = route_scores / jnp.sum(route_scores, axis=1, keepdims=True)
    coef = jnp.sum(jnp.where(named, shares[:, :, None], F32(0.0)), axis=1)
    order = jnp.arange(rows_here, dtype=jnp.int32)
    before = (order[None, :] < order[:, None]).astype(BF)
    rank = jnp.dot(before, chosen.astype(BF), preferred_element_type=F32).astype(jnp.int32)
    taken = chosen[:, :, None] & (rank[:, :, None] == jnp.arange(capacity, dtype=jnp.int32))
    slots = experts * capacity
    pick = taken.reshape(rows_here, slots).astype(BF)
    mixing = jnp.where(taken, coef[:, :, None], F32(0.0)).reshape(rows_here, slots)

    outgoing = lax.dot_general(
        pick, scaled, (((0,), (0,)), ((), ())), preferred_element_type=F32
    ).astype(BF)
    outgoing = outgoing.reshape(roles * shards, per_dev * capacity, half)
    incoming = lax.all_to_all(outgoing, ("role", "rows"), 0, 0, tiled=True)
    incoming = incoming.reshape(roles, shards, per_dev, capacity, half)

    plain = incoming.astype(F32) / norm_gain.reshape(roles, 1, 1, 1, half)
    meansq = jnp.sum(plain * plain, axis=(0, 4)) / width
    inverse = lax.rsqrt(meansq + EPS)
    inverse = inverse.transpose(1, 0, 2).reshape(per_dev, shards * capacity, 1)
    tokens = incoming.transpose(2, 0, 1, 3, 4).reshape(per_dev, roles, shards * capacity, half)

    def project(weight):
        weight = weight.reshape(per_dev, roles, half, quarter)
        value = jnp.einsum("esd,edf->esf", tokens[:, 0], weight[:, 0], preferred_element_type=F32)
        for s in range(1, roles):
            value = value + jnp.einsum(
                "esd,edf->esf", tokens[:, s], weight[:, s], preferred_element_type=F32
            )
        return value * inverse

    act = (jax.nn.silu(project(w_gate)) * project(w_up)).astype(BF)
    result = jnp.einsum("esf,efd->esd", act, downs[0], preferred_element_type=F32)
    for step in range(1, heads_count):
        result = result + jnp.einsum(
            "esf,efd->esd", shift(act, step), downs[step], preferred_element_type=F32
        )
    result = result.astype(BF).reshape(per_dev, shards, capacity, roles, piece)
    result = result.transpose(3, 1, 0, 2, 4).reshape(roles * shards, per_dev * capacity, piece)
    returned = lax.all_to_all(result, ("role", "rows"), 0, 0, tiled=True)
    returned = returned.reshape(slots, piece)
    mix_high = mixing.astype(BF)
    mix_low = (mixing - mix_high.astype(F32)).astype(BF)
    moe = jnp.dot(mix_high, returned, preferred_element_type=F32) + jnp.dot(
        mix_low, returned, preferred_element_type=F32
    )
    own = lax.dynamic_slice_in_dim(hidden, head * piece, piece, 1)
    return (own + moe).astype(BF)


def solution(mesh):
    in_specs = (
        P("rows", "role", "heads", None),
        P("rows", "heads", None, None),
        P("rows", "heads", None, None),
        P("rows", "heads", None),
        P("rows", "heads", None),
        P("rows"),
        P("role", "heads", None, None),
        P("rows", None),
        P(),
        P("rows", None),
        P("rows", None),
        P(("role", "rows"), None, "heads"),
        P(("role", "rows"), None, "heads"),
        P(("role", "rows"), "heads", None),
    )
    out_specs = P("rows", ("role", "heads"))
    return jax.shard_map(
        per_device, mesh=mesh, in_specs=in_specs, out_specs=out_specs, check_vma=False
    )
```

```python
import math

import jax
import jax.numpy as jnp
from jax import lax
from jax.experimental import pallas as pl
from jax.experimental.pallas import tpu as pltpu
from jax.sharding import PartitionSpec as P

BF = jnp.bfloat16
F32 = jnp.float32
EPS = 1e-06
VMEM = 60 << 20


def whole(n):
    return [pl.BlockSpec(memory_space=pltpu.VMEM)] * n


def cut_down(w_down, head, heads_count, roles):
    per_dev, quarter, width = w_down.shape
    half = width // roles
    piece = half // heads_count

    def body(head_ref, w_ref, *rest):
        outs, sems = rest[:heads_count], rest[heads_count]
        copies = []
        for step in range(heads_count):
            place = lax.rem(head_ref[0] + step, heads_count)
            for s in range(roles):
                start = pl.multiple_of(s * half + place * piece, piece)
                copies.append(
                    pltpu.make_async_copy(
                        w_ref.at[:, :, pl.ds(start, piece)],
                        outs[step].at[:, :, pl.ds(s * piece, piece)],
                        sems.at[step * roles + s],
                    )
                )
        for copy in copies:
            copy.start()
        for copy in copies:
            copy.wait()

    shape = jax.ShapeDtypeStruct((per_dev, quarter, roles * piece), w_down.dtype)
    return pl.pallas_call(
        body,
        out_shape=[shape] * heads_count,
        in_specs=[pl.BlockSpec(memory_space=pltpu.SMEM), pl.BlockSpec(memory_space=pltpu.HBM)],
        out_specs=[pl.BlockSpec(memory_space=pltpu.HBM)] * heads_count,
        scratch_shapes=[pltpu.SemaphoreType.DMA((heads_count * roles,))],
        compiler_params=pltpu.CompilerParams(vmem_limit_bytes=VMEM),
        cost_estimate=pl.CostEstimate(
            flops=0, bytes_accessed=2 * w_down.size * 2, transcendentals=0
        ),
        name="cut_down",
    )(head.reshape(1), w_down)


def attend(queries, k_cache, value_cache, new_key, new_value, lengths, output_weight, other):
    rows, group, size = queries.shape
    cache = k_cache.shape[1]
    depth, width = output_weight.shape
    half = width // 2
    step = 8
    blocks = rows // step
    scale = 1.0 / math.sqrt(size)

    def body(
        other_ref, q_ref, k_hbm, v_hbm, nk_ref, nv_ref, len_ref, w_hbm,
        attn_ref, out_ref, k_ref, v_ref, w_ref, k_sem, v_sem, w_sem,
    ):
        def copy(hbm, ref, sem, i):
            place = pl.ds(i * step, step)
            return pltpu.make_async_copy(hbm.at[place], ref.at[place], sem.at[i])

        start = pl.multiple_of(other_ref[0] * half, half)
        weight = pltpu.make_async_copy(w_hbm.at[:, pl.ds(start, half)], w_ref, w_sem)
        for i in range(blocks):
            copy(k_hbm, k_ref, k_sem, i).start()
            copy(v_hbm, v_ref, v_sem, i).start()
        weight.start()
        for i in range(blocks):
            place = slice(i * step, (i + 1) * step)
            copy(k_hbm, k_ref, k_sem, i).wait()
            q = q_ref[place]
            scores = lax.dot_general(
                q, k_ref[place], (((2,), (2,)), ((0,), (0,))), preferred_element_type=F32
            )
            scores = scores * scale
            fresh = jnp.sum(
                q.astype(F32) * nk_ref[place].astype(F32)[:, None, :], axis=2, keepdims=True
            )
            fresh = fresh * scale
            position = lax.broadcasted_iota(jnp.int32, (step, group, cache), 2)
            limit = len_ref[place][:, :, None]
            scores = jnp.where(position < limit, scores, -jnp.inf)
            top = jnp.maximum(jnp.max(scores, axis=2, keepdims=True), fresh)
            expo = jnp.exp(scores - top)
            expo_new = jnp.exp(fresh - top)
            denom = jnp.sum(expo, axis=2, keepdims=True) + expo_new
            probs = (expo / denom).astype(BF)
            probs_new = (expo_new / denom).astype(BF).astype(F32)
            copy(v_hbm, v_ref, v_sem, i).wait()
            result = lax.dot_general(
                probs, v_ref[place], (((2,), (1,)), ((0,), (0,))), preferred_element_type=F32
            )
            result = result + probs_new * nv_ref[place].astype(F32)[:, None, :]
            attn_ref[place, :] = result.reshape(step, group * size).astype(BF)
        weight.wait()
        out_ref[...] = jnp.dot(
            attn_ref[...], w_ref[...], preferred_element_type=F32
        ).astype(BF)

    return pl.pallas_call(
        body,
        out_shape=[
            jax.ShapeDtypeStruct((rows, depth), BF),
            jax.ShapeDtypeStruct((rows, half), BF),
        ],
        in_specs=[
            pl.BlockSpec(memory_space=pltpu.SMEM),
            pl.BlockSpec(memory_space=pltpu.VMEM),
            pl.BlockSpec(memory_space=pltpu.HBM),
            pl.BlockSpec(memory_space=pltpu.HBM),
            pl.BlockSpec(memory_space=pltpu.VMEM),
            pl.BlockSpec(memory_space=pltpu.VMEM),
            pl.BlockSpec(memory_space=pltpu.VMEM),
            pl.BlockSpec(memory_space=pltpu.HBM),
        ],
        out_specs=whole(2),
        scratch_shapes=[
            pltpu.VMEM((rows, cache, size), BF),
            pltpu.VMEM((rows, cache, size), BF),
            pltpu.VMEM((depth, half), BF),
            pltpu.SemaphoreType.DMA((blocks,)),
            pltpu.SemaphoreType.DMA((blocks,)),
            pltpu.SemaphoreType.DMA,
        ],
        compiler_params=pltpu.CompilerParams(vmem_limit_bytes=57 << 20),
        cost_estimate=pl.CostEstimate(
            flops=2 * rows * depth * half, bytes_accessed=12 << 20, transcendentals=0
        ),
        name="attend",
    )(other.reshape(1), queries, k_cache, value_cache, new_key, new_value, lengths, output_weight)


def own_half(attended, output_weight, role):
    rows = attended.shape[0]
    depth, width = output_weight.shape
    half = width // 2

    def body(role_ref, a_ref, w_hbm, out_ref, w_ref, sem):
        start = pl.multiple_of(role_ref[0] * half, half)
        copy = pltpu.make_async_copy(w_hbm.at[:, pl.ds(start, half)], w_ref, sem)
        copy.start()
        copy.wait()
        out_ref[...] = jnp.dot(a_ref[...], w_ref[...], preferred_element_type=F32)

    return pl.pallas_call(
        body,
        out_shape=jax.ShapeDtypeStruct((rows, half), F32),
        in_specs=[
            pl.BlockSpec(memory_space=pltpu.SMEM),
            pl.BlockSpec(memory_space=pltpu.VMEM),
            pl.BlockSpec(memory_space=pltpu.HBM),
        ],
        out_specs=pl.BlockSpec(memory_space=pltpu.VMEM),
        scratch_shapes=[pltpu.VMEM((depth, half), BF), pltpu.SemaphoreType.DMA],
        compiler_params=pltpu.CompilerParams(vmem_limit_bytes=57 << 20),
        cost_estimate=pl.CostEstimate(
            flops=2 * rows * depth * half, bytes_accessed=4 << 20, transcendentals=0
        ),
        name="own_half",
    )(role.reshape(1), attended, output_weight)


def experts_act(tokens, gain, w_gate, w_up, capacity):
    roles, slots, half = tokens.shape
    per_dev, width, quarter = w_gate.shape

    def body(x_ref, gain_ref, g_hbm, u_hbm, act_ref, g_ref, u_ref, sems):
        copies = []
        for e in range(per_dev):
            for i, (hbm, ref) in enumerate(((g_hbm, g_ref), (u_hbm, u_ref))):
                copies.append(pltpu.make_async_copy(hbm.at[e], ref.at[e], sems.at[2 * e + i]))
        for copy in copies:
            copy.start()
        square = jnp.zeros((slots, 1), F32)
        for s in range(roles):
            plain = x_ref[s].astype(F32) / gain_ref[s]
            square = square + jnp.sum(plain * plain, axis=1, keepdims=True)
        inverse = lax.rsqrt(square / width + EPS)

        def product(w_ref, e):
            value = jnp.dot(x_ref[0], w_ref[e, :half], preferred_element_type=F32)
            for s in range(1, roles):
                value = value + jnp.dot(
                    x_ref[s], w_ref[e, s * half : (s + 1) * half], preferred_element_type=F32
                )
            return value

        expert = lax.broadcasted_iota(jnp.int32, (slots, 1), 0) // capacity % per_dev
        gate = upper = jnp.zeros((slots, quarter), F32)
        for e in range(per_dev):
            copies[2 * e].wait()
            gate = jnp.where(expert == e, product(g_ref, e), gate)
            copies[2 * e + 1].wait()
            upper = jnp.where(expert == e, product(u_ref, e), upper)
        gate, upper = gate * inverse, upper * inverse
        act_ref[...] = (gate / (1.0 + jnp.exp(-gate)) * upper).astype(BF)

    return pl.pallas_call(
        body,
        out_shape=jax.ShapeDtypeStruct((slots, quarter), BF),
        in_specs=whole(2) + [pl.BlockSpec(memory_space=pltpu.HBM)] * 2,
        out_specs=pl.BlockSpec(memory_space=pltpu.VMEM),
        scratch_shapes=[
            pltpu.VMEM(w_gate.shape, BF),
            pltpu.VMEM(w_up.shape, BF),
            pltpu.SemaphoreType.DMA((2 * per_dev,)),
        ],
        compiler_params=pltpu.CompilerParams(vmem_limit_bytes=57 << 20),
        cost_estimate=pl.CostEstimate(
            flops=4 * per_dev * slots * width * quarter,
            bytes_accessed=10 << 20,
            transcendentals=0,
        ),
        name="experts_act",
    )(tokens, gain, w_gate, w_up)


def experts_down(acts, downs, capacity, roles):
    count = len(acts)
    slots, quarter = acts[0].shape
    per_dev, _, columns = downs[0].shape
    piece = columns // roles

    def body(*refs):
        a_refs, w_refs, out_ref = refs[:count], refs[count : 2 * count], refs[2 * count]
        expert = lax.broadcasted_iota(jnp.int32, (slots, 1), 0) // capacity % per_dev
        zero = jnp.zeros((slots, quarter), BF)
        for s in range(roles):
            total = jnp.zeros((slots, piece), F32)
            for a_ref, w_ref in zip(a_refs, w_refs):
                for e in range(per_dev):
                    total = total + jnp.dot(
                        jnp.where(expert == e, a_ref[...], zero),
                        w_ref[e, :, s * piece : (s + 1) * piece],
                        preferred_element_type=F32,
                    )
            out_ref[s * slots : (s + 1) * slots] = total.astype(BF)

    return pl.pallas_call(
        body,
        out_shape=jax.ShapeDtypeStruct((roles * slots, piece), BF),
        in_specs=whole(2 * count),
        out_specs=pl.BlockSpec(memory_space=pltpu.VMEM),
        compiler_params=pltpu.CompilerParams(vmem_limit_bytes=24 << 20),
        cost_estimate=pl.CostEstimate(
            flops=2 * slots * count * per_dev * quarter * columns,
            bytes_accessed=5 << 20,
            transcendentals=0,
        ),
        name="experts_down",
    )(*acts, *downs)


def per_device(
    queries,
    k_cache,
    value_cache,
    new_token_key,
    new_token_value,
    lengths,
    output_weight,
    residual,
    norm_gain,
    routes,
    route_scores,
    w_gate,
    w_up,
    w_down,
):
    rows_here = queries.shape[0]
    width = residual.shape[1]
    roles = lax.axis_size("role")
    heads_count = lax.axis_size("heads")
    shards = lax.axis_size("rows")
    half = width // roles
    piece = half // heads_count
    per_dev, _, quarter = w_gate.shape
    experts = per_dev * shards * roles
    capacity = 8
    role = lax.axis_index("role")
    head = lax.axis_index("heads")
    swap = [(i, roles - 1 - i) for i in range(roles)]

    def shift(x, step):
        return lax.ppermute(
            x, "heads", [(i, (i + step) % heads_count) for i in range(heads_count)]
        )

    downs = cut_down(w_down, head, heads_count, roles)

    head_size = k_cache.shape[3]
    query_vectors = queries.reshape(rows_here, -1, head_size)
    attended, theirs = attend(
        query_vectors,
        k_cache[:, 0],
        value_cache[:, 0],
        new_token_key[:, 0],
        new_token_value[:, 0],
        lengths.reshape(rows_here, 1),
        output_weight[0, 0],
        1 - role,
    )
    received = lax.ppermute(theirs, "role", swap)
    mine = own_half(attended, output_weight[0, 0], role)
    chip = (mine + received.astype(F32)).astype(BF)
    total = chip.astype(F32)
    for step in range(1, heads_count):
        total = total + shift(chip, step).astype(F32)
    first = role == 0
    resid = jnp.where(first, residual[:, :half], residual[:, half:]).astype(F32)
    gain = jnp.where(first, norm_gain[:half], norm_gain[half:])
    hidden = resid + total
    hidden, *downs = lax.optimization_barrier((hidden, *downs))
    downs = [w if step == 0 else shift(w, step) for step, w in enumerate(downs)]
    scaled = (hidden * gain).astype(BF)

    named = routes[:, :, None] == jnp.arange(experts, dtype=jnp.int32)
    chosen = jnp.any(named, axis=1)
    shares = route_scores / jnp.sum(route_scores, axis=1, keepdims=True)
    coef = jnp.sum(jnp.where(named, shares[:, :, None], F32(0.0)), axis=1)
    order = jnp.arange(rows_here, dtype=jnp.int32)
    before = (order[None, :] < order[:, None]).astype(BF)
    rank = jnp.dot(before, chosen.astype(BF), preferred_element_type=F32).astype(jnp.int32)
    taken = chosen[:, :, None] & (rank[:, :, None] == jnp.arange(capacity, dtype=jnp.int32))
    slots = experts * capacity
    pick = taken.reshape(rows_here, slots).astype(BF)
    mixing = jnp.where(taken, coef[:, :, None], F32(0.0)).reshape(rows_here, slots)

    outgoing = lax.dot_general(
        pick, scaled, (((0,), (0,)), ((), ())), preferred_element_type=F32
    ).astype(BF)
    outgoing = outgoing.reshape(roles * shards, per_dev * capacity, half)
    incoming = lax.all_to_all(outgoing, ("role", "rows"), 0, 0, tiled=True)
    tokens = incoming.reshape(roles, shards * per_dev * capacity, half)
    act = experts_act(tokens, norm_gain.reshape(roles, 1, half), w_gate, w_up, capacity)
    acts = [act if step == 0 else shift(act, step) for step in range(heads_count)]
    result = experts_down(acts, downs, capacity, roles)
    result = result.reshape(roles * shards, per_dev * capacity, piece)
    returned = lax.all_to_all(result, ("role", "rows"), 0, 0, tiled=True)
    returned = returned.reshape(slots, piece)
    mix_high = mixing.astype(BF)
    mix_low = (mixing - mix_high.astype(F32)).astype(BF)
    moe = jnp.dot(mix_high, returned, preferred_element_type=F32) + jnp.dot(
        mix_low, returned, preferred_element_type=F32
    )
    own = lax.dynamic_slice_in_dim(hidden, head * piece, piece, 1)
    return (own + moe).astype(BF)


def solution(mesh):
    in_specs = (
        P("rows", "role", "heads", None),
        P("rows", "heads", None, None),
        P("rows", "heads", None, None),
        P("rows", "heads", None),
        P("rows", "heads", None),
        P("rows"),
        P("role", "heads", None, None),
        P("rows", None),
        P(),
        P("rows", None),
        P("rows", None),
        P(("role", "rows"), None, "heads"),
        P(("role", "rows"), None, "heads"),
        P(("role", "rows"), "heads", None),
    )
    out_specs = P("rows", ("role", "heads"))
    return jax.shard_map(
        per_device, mesh=mesh, in_specs=in_specs, out_specs=out_specs, check_vma=False
    )
```

```python
import math

import jax
import jax.numpy as jnp
from jax import lax
from jax.experimental import pallas as pl
from jax.experimental.pallas import tpu as pltpu
from jax.sharding import PartitionSpec as P

BF = jnp.bfloat16
F32 = jnp.float32
EPS = 1e-06
VMEM = 60 << 20


def whole(n):
    return [pl.BlockSpec(memory_space=pltpu.VMEM)] * n


def cut_down(w_down, head, heads_count, roles):
    per_dev, quarter, width = w_down.shape
    half = width // roles
    piece = half // heads_count
    parts = 4

    def body(head_ref, w_hbm, *rest):
        outs, w_ref, in_sems, out_sems = rest[:heads_count], *rest[heads_count:]
        loads, stores = [], []
        for e in range(per_dev):
            for i in range(parts):
                rows = pl.ds(i * (quarter // parts), quarter // parts)
                loads.append(
                    pltpu.make_async_copy(
                        w_hbm.at[e, rows], w_ref.at[e, rows], in_sems.at[e * parts + i]
                    )
                )
            for step in range(heads_count):
                place = lax.rem(head_ref[0] + step, heads_count)
                for s in range(roles):
                    start = pl.multiple_of(s * half + place * piece, piece)
                    stores.append(
                        pltpu.make_async_copy(
                            w_ref.at[e, :, pl.ds(start, piece)],
                            outs[step].at[e, :, pl.ds(s * piece, piece)],
                            out_sems.at[(e * heads_count + step) * roles + s],
                        )
                    )
        for load in loads:
            load.start()
        for e in range(per_dev):
            for load in loads[e * parts : (e + 1) * parts]:
                load.wait()
            each = heads_count * roles
            for store in stores[e * each : (e + 1) * each]:
                store.start()
        for store in stores:
            store.wait()

    shape = jax.ShapeDtypeStruct((per_dev, quarter, roles * piece), w_down.dtype)
    return pl.pallas_call(
        body,
        out_shape=[shape] * heads_count,
        in_specs=[pl.BlockSpec(memory_space=pltpu.SMEM), pl.BlockSpec(memory_space=pltpu.HBM)],
        out_specs=[pl.BlockSpec(memory_space=pltpu.HBM)] * heads_count,
        scratch_shapes=[
            pltpu.VMEM(w_down.shape, BF),
            pltpu.SemaphoreType.DMA((per_dev * parts,)),
            pltpu.SemaphoreType.DMA((per_dev * heads_count * roles,)),
        ],
        compiler_params=pltpu.CompilerParams(vmem_limit_bytes=VMEM),
        cost_estimate=pl.CostEstimate(
            flops=0, bytes_accessed=2 * w_down.size * 2, transcendentals=0
        ),
        name="cut_down",
    )(head.reshape(1), w_down)


def attend(queries, k_cache, value_cache, new_key, new_value, lengths, output_weight, role):
    rows, depth = queries.shape
    cache, size = k_cache.shape[1:]
    group = depth // size
    width = output_weight.shape[1]
    half = width // 2
    step = 8
    blocks = rows // step
    scale = 1.0 / math.sqrt(size)

    def body(
        role_ref, len_ref, q_ref, k_hbm, v_hbm, nk_ref, nv_ref, w_hbm,
        theirs_ref, mine_ref, k_ref, v_ref, w_ref, attn_ref, k_sem, v_sem, w_sem,
    ):
        def copy(hbm, ref, sem, i):
            place = pl.ds(i * step, step)
            return pltpu.make_async_copy(hbm.at[place], ref.at[place], sem.at[i])

        weights = []
        for s in range(2):
            side = role_ref[0] if s else 1 - role_ref[0]
            start = pl.multiple_of(side * half, half)
            for i in range(4):
                place = pl.ds(i * (depth // 4), depth // 4)
                weights.append(
                    pltpu.make_async_copy(
                        w_hbm.at[place, pl.ds(start, half)],
                        w_ref.at[s, place],
                        w_sem.at[4 * s + i],
                    )
                )
        for i in range(blocks):
            copy(k_hbm, k_ref, k_sem, i).start()
            copy(v_hbm, v_ref, v_sem, i).start()
        for weight in weights:
            weight.start()
        for i in range(blocks):
            place = slice(i * step, (i + 1) * step)
            q = q_ref[place].reshape(step, group, size)
            copy(k_hbm, k_ref, k_sem, i).wait()
            scores = lax.dot_general(
                q, k_ref[place], (((2,), (2,)), ((0,), (0,))), preferred_element_type=F32
            )
            scores = scores * scale
            fresh = jnp.sum(
                q.astype(F32) * nk_ref[place].astype(F32)[:, None, :], axis=2, keepdims=True
            )
            fresh = fresh * scale
            position = lax.broadcasted_iota(jnp.int32, (step, group, cache), 2)
            row = lax.broadcasted_iota(jnp.int32, (step, group, cache), 0)
            limit = jnp.full((step, group, cache), len_ref[i * step])
            for j in range(1, step):
                limit = jnp.where(row == j, len_ref[i * step + j], limit)
            scores = jnp.where(position < limit, scores, -jnp.inf)
            top = jnp.maximum(jnp.max(scores, axis=2, keepdims=True), fresh)
            expo = jnp.exp(scores - top)
            expo_new = jnp.exp(fresh - top)
            inverse = 1.0 / (jnp.sum(expo, axis=2, keepdims=True) + expo_new)
            probs = (expo * inverse).astype(BF)
            probs_new = (expo_new * inverse).astype(BF).astype(F32)
            copy(v_hbm, v_ref, v_sem, i).wait()
            result = lax.dot_general(
                probs, v_ref[place], (((2,), (1,)), ((0,), (0,))), preferred_element_type=F32
            )
            result = result + probs_new * nv_ref[place].astype(F32)[:, None, :]
            attn_ref[place, :] = result.reshape(step, depth).astype(BF)
        for weight in weights[:4]:
            weight.wait()
        product = jnp.dot(attn_ref[...], w_ref[0], preferred_element_type=F32)
        theirs_ref[...] = product.astype(BF)
        for weight in weights[4:]:
            weight.wait()
        mine_ref[...] = jnp.dot(attn_ref[...], w_ref[1], preferred_element_type=F32)

    return pl.pallas_call(
        body,
        out_shape=[
            jax.ShapeDtypeStruct((rows, half), BF),
            jax.ShapeDtypeStruct((rows, half), F32),
        ],
        in_specs=[
            pl.BlockSpec(memory_space=pltpu.SMEM),
            pl.BlockSpec(memory_space=pltpu.SMEM),
            pl.BlockSpec(memory_space=pltpu.VMEM),
            pl.BlockSpec(memory_space=pltpu.HBM),
            pl.BlockSpec(memory_space=pltpu.HBM),
            pl.BlockSpec(memory_space=pltpu.VMEM),
            pl.BlockSpec(memory_space=pltpu.VMEM),
            pl.BlockSpec(memory_space=pltpu.HBM),
        ],
        out_specs=whole(2),
        scratch_shapes=[
            pltpu.VMEM((rows, cache, size), BF),
            pltpu.VMEM((rows, cache, size), BF),
            pltpu.VMEM((2, depth, half), BF),
            pltpu.VMEM((rows, depth), BF),
            pltpu.SemaphoreType.DMA((blocks,)),
            pltpu.SemaphoreType.DMA((blocks,)),
            pltpu.SemaphoreType.DMA((8,)),
        ],
        compiler_params=pltpu.CompilerParams(vmem_limit_bytes=57 << 20),
        cost_estimate=pl.CostEstimate(
            flops=2 * rows * depth * width, bytes_accessed=16 << 20, transcendentals=0
        ),
        name="attend",
    )(role.reshape(1), lengths, queries, k_cache, value_cache, new_key, new_value, output_weight)


def experts_act(tokens, gain, w_gate, w_up, capacity):
    roles, slots, half = tokens.shape
    per_dev, width, quarter = w_gate.shape

    def body(x_ref, gain_ref, g_hbm, u_hbm, act_ref, g_ref, u_ref, sems):
        copies = []
        for e in range(per_dev):
            for i, (hbm, ref) in enumerate(((g_hbm, g_ref), (u_hbm, u_ref))):
                copies.append(pltpu.make_async_copy(hbm.at[e], ref.at[e], sems.at[2 * e + i]))
        for copy in copies:
            copy.start()
        square = jnp.zeros((slots, 1), F32)
        for s in range(roles):
            plain = x_ref[s].astype(F32) * (1.0 / gain_ref[s])
            square = square + jnp.sum(plain * plain, axis=1, keepdims=True)
        inverse = lax.rsqrt(square / width + EPS)

        def product(w_ref, e):
            value = jnp.dot(x_ref[0], w_ref[e, :half], preferred_element_type=F32)
            for s in range(1, roles):
                value = value + jnp.dot(
                    x_ref[s], w_ref[e, s * half : (s + 1) * half], preferred_element_type=F32
                )
            return value

        expert = lax.broadcasted_iota(jnp.int32, (slots, 1), 0) // capacity % per_dev
        gate = upper = jnp.zeros((slots, quarter), F32)
        for e in range(per_dev):
            copies[2 * e].wait()
            gate = jnp.where(expert == e, product(g_ref, e), gate)
            copies[2 * e + 1].wait()
            upper = jnp.where(expert == e, product(u_ref, e), upper)
        gate, upper = gate * inverse, upper * inverse
        act_ref[...] = (gate / (1.0 + jnp.exp(-gate)) * upper).astype(BF)

    return pl.pallas_call(
        body,
        out_shape=jax.ShapeDtypeStruct((slots, quarter), BF),
        in_specs=whole(2) + [pl.BlockSpec(memory_space=pltpu.HBM)] * 2,
        out_specs=pl.BlockSpec(memory_space=pltpu.VMEM),
        scratch_shapes=[
            pltpu.VMEM(w_gate.shape, BF),
            pltpu.VMEM(w_up.shape, BF),
            pltpu.SemaphoreType.DMA((2 * per_dev,)),
        ],
        compiler_params=pltpu.CompilerParams(vmem_limit_bytes=57 << 20),
        cost_estimate=pl.CostEstimate(
            flops=4 * per_dev * slots * width * quarter,
            bytes_accessed=10 << 20,
            transcendentals=0,
        ),
        name="experts_act",
    )(tokens, gain, w_gate, w_up)


def experts_down(acts, downs, capacity, roles):
    count = len(acts)
    slots, quarter = acts[0].shape
    per_dev, _, columns = downs[0].shape
    piece = columns // roles

    def body(*refs):
        a_refs, w_refs, out_ref = refs[:count], refs[count : 2 * count], refs[2 * count]
        expert = lax.broadcasted_iota(jnp.int32, (slots, 1), 0) // capacity % per_dev
        zero = jnp.zeros((slots, quarter), BF)
        for s in range(roles):
            total = jnp.zeros((slots, piece), F32)
            for a_ref, w_ref in zip(a_refs, w_refs):
                for e in range(per_dev):
                    total = total + jnp.dot(
                        jnp.where(expert == e, a_ref[...], zero),
                        w_ref[e, :, s * piece : (s + 1) * piece],
                        preferred_element_type=F32,
                    )
            out_ref[s * slots : (s + 1) * slots] = total.astype(BF)

    return pl.pallas_call(
        body,
        out_shape=jax.ShapeDtypeStruct((roles * slots, piece), BF),
        in_specs=whole(2 * count),
        out_specs=pl.BlockSpec(memory_space=pltpu.VMEM),
        compiler_params=pltpu.CompilerParams(vmem_limit_bytes=24 << 20),
        cost_estimate=pl.CostEstimate(
            flops=2 * slots * count * per_dev * quarter * columns,
            bytes_accessed=5 << 20,
            transcendentals=0,
        ),
        name="experts_down",
    )(*acts, *downs)


def per_device(
    queries,
    k_cache,
    value_cache,
    new_token_key,
    new_token_value,
    lengths,
    output_weight,
    residual,
    norm_gain,
    routes,
    route_scores,
    w_gate,
    w_up,
    w_down,
):
    rows_here = queries.shape[0]
    width = residual.shape[1]
    roles = lax.axis_size("role")
    heads_count = lax.axis_size("heads")
    shards = lax.axis_size("rows")
    half = width // roles
    piece = half // heads_count
    per_dev, _, quarter = w_gate.shape
    experts = per_dev * shards * roles
    capacity = 8
    role = lax.axis_index("role")
    head = lax.axis_index("heads")
    swap = [(i, roles - 1 - i) for i in range(roles)]

    def shift(x, step):
        return lax.ppermute(
            x, "heads", [(i, (i + step) % heads_count) for i in range(heads_count)]
        )

    theirs, mine = attend(
        queries[:, 0, 0],
        k_cache[:, 0],
        value_cache[:, 0],
        new_token_key[:, 0],
        new_token_value[:, 0],
        lengths,
        output_weight[0, 0],
        role,
    )
    received = lax.ppermute(theirs, "role", swap)
    chip, w_down = lax.optimization_barrier(((mine + received.astype(F32)).astype(BF), w_down))
    downs = cut_down(w_down, head, heads_count, roles)
    total = chip.astype(F32)
    for step in range(1, heads_count):
        total = total + shift(chip, step).astype(F32)
    first = role == 0
    resid = jnp.where(first, residual[:, :half], residual[:, half:]).astype(F32)
    gain = jnp.where(first, norm_gain[:half], norm_gain[half:])
    hidden = resid + total
    hidden, *downs = lax.optimization_barrier((hidden, *downs))
    downs = [w if step == 0 else shift(w, step) for step, w in enumerate(downs)]
    scaled = (hidden * gain).astype(BF)

    named = routes[:, :, None] == jnp.arange(experts, dtype=jnp.int32)
    chosen = jnp.any(named, axis=1)
    shares = route_scores / jnp.sum(route_scores, axis=1, keepdims=True)
    coef = jnp.sum(jnp.where(named, shares[:, :, None], F32(0.0)), axis=1)
    order = jnp.arange(rows_here, dtype=jnp.int32)
    before = (order[None, :] < order[:, None]).astype(BF)
    rank = jnp.dot(before, chosen.astype(BF), preferred_element_type=F32).astype(jnp.int32)
    taken = chosen[:, :, None] & (rank[:, :, None] == jnp.arange(capacity, dtype=jnp.int32))
    slots = experts * capacity
    pick = taken.reshape(rows_here, slots).astype(BF)
    mixing = jnp.where(taken, coef[:, :, None], F32(0.0)).reshape(rows_here, slots)

    outgoing = lax.dot_general(
        pick, scaled, (((0,), (0,)), ((), ())), preferred_element_type=F32
    ).astype(BF)
    outgoing = outgoing.reshape(roles * shards, per_dev * capacity, half)
    incoming = lax.all_to_all(outgoing, ("role", "rows"), 0, 0, tiled=True)
    tokens = incoming.reshape(roles, shards * per_dev * capacity, half)
    act = experts_act(tokens, norm_gain.reshape(roles, 1, half), w_gate, w_up, capacity)
    acts = [act if step == 0 else shift(act, step) for step in range(heads_count)]
    result = experts_down(acts, downs, capacity, roles)
    result = result.reshape(roles * shards, per_dev * capacity, piece)
    returned = lax.all_to_all(result, ("role", "rows"), 0, 0, tiled=True)
    returned = returned.reshape(slots, piece)
    mix_high = mixing.astype(BF)
    mix_low = (mixing - mix_high.astype(F32)).astype(BF)
    moe = jnp.dot(mix_high, returned, preferred_element_type=F32) + jnp.dot(
        mix_low, returned, preferred_element_type=F32
    )
    own = lax.dynamic_slice_in_dim(hidden, head * piece, piece, 1)
    return (own + moe).astype(BF)


def solution(mesh):
    in_specs = (
        P("rows", "role", "heads", None),
        P("rows", "heads", None, None),
        P("rows", "heads", None, None),
        P("rows", "heads", None),
        P("rows", "heads", None),
        P("rows"),
        P("role", "heads", None, None),
        P("rows", None),
        P(),
        P("rows", None),
        P("rows", None),
        P(("role", "rows"), None, "heads"),
        P(("role", "rows"), None, "heads"),
        P(("role", "rows"), "heads", None),
    )
    out_specs = P("rows", ("role", "heads"))
    return jax.shard_map(
        per_device, mesh=mesh, in_specs=in_specs, out_specs=out_specs, check_vma=False
    )
```

```python
import math

import jax
import jax.numpy as jnp
from jax import lax
from jax.experimental import pallas as pl
from jax.experimental.pallas import tpu as pltpu
from jax.sharding import PartitionSpec as P

BF = jnp.bfloat16
F32 = jnp.float32
EPS = 1e-06
VMEM = 60 << 20


def whole(n):
    return [pl.BlockSpec(memory_space=pltpu.VMEM)] * n


def cut_down(w_down, head, heads_count, roles, pieces):
    per_dev, quarter, width = w_down.shape
    half = width // roles
    piece = half // heads_count
    parts = 4
    count = len(pieces)

    def body(head_ref, w_hbm, *rest):
        outs, w_ref, in_sems, out_sems = rest[:count], *rest[count:]
        loads, stores = [], []
        for e in range(per_dev):
            for i in range(parts):
                rows = pl.ds(i * (quarter // parts), quarter // parts)
                loads.append(
                    pltpu.make_async_copy(
                        w_hbm.at[e, rows], w_ref.at[e, rows], in_sems.at[e * parts + i]
                    )
                )
        for i, (step, e) in enumerate(pieces):
            place = lax.rem(head_ref[0] + step, heads_count)
            for s in range(roles):
                start = pl.multiple_of(s * half + place * piece, piece)
                stores.append(
                    pltpu.make_async_copy(
                        w_ref.at[e, :, pl.ds(start, piece)],
                        outs[i].at[:, pl.ds(s * piece, piece)],
                        out_sems.at[i * roles + s],
                    )
                )
        for load in loads:
            load.start()
        for e in range(per_dev):
            for load in loads[e * parts : (e + 1) * parts]:
                load.wait()
            for i, (_, mine) in enumerate(pieces):
                if mine == e:
                    for store in stores[i * roles : (i + 1) * roles]:
                        store.start()
        for store in stores:
            store.wait()

    return pl.pallas_call(
        body,
        out_shape=[jax.ShapeDtypeStruct((quarter, roles * piece), BF)] * count,
        in_specs=[pl.BlockSpec(memory_space=pltpu.SMEM), pl.BlockSpec(memory_space=pltpu.HBM)],
        out_specs=[pl.BlockSpec(memory_space=pltpu.HBM)] * count,
        scratch_shapes=[
            pltpu.VMEM(w_down.shape, BF),
            pltpu.SemaphoreType.DMA((per_dev * parts,)),
            pltpu.SemaphoreType.DMA((count * roles,)),
        ],
        compiler_params=pltpu.CompilerParams(vmem_limit_bytes=VMEM),
        cost_estimate=pl.CostEstimate(
            flops=0, bytes_accessed=2 * w_down.size * 2, transcendentals=0
        ),
        name="cut_down",
    )(head.reshape(1), w_down)


def attend(queries, k_cache, value_cache, new_key, new_value, lengths, output_weight, role):
    rows, depth = queries.shape
    cache, size = k_cache.shape[1:]
    group = depth // size
    width = output_weight.shape[1]
    half = width // 2
    step = 8
    blocks = rows // step
    scale = 1.0 / math.sqrt(size)

    def body(
        role_ref, len_ref, q_ref, k_hbm, v_hbm, nk_ref, nv_ref, w_hbm,
        theirs_ref, mine_ref, k_ref, v_ref, w_ref, attn_ref, k_sem, v_sem, w_sem,
    ):
        def copy(hbm, ref, sem, i):
            place = pl.ds(i * step, step)
            return pltpu.make_async_copy(hbm.at[place], ref.at[place], sem.at[i])

        weights = []
        for s in range(2):
            side = role_ref[0] if s else 1 - role_ref[0]
            start = pl.multiple_of(side * half, half)
            for i in range(4):
                place = pl.ds(i * (depth // 4), depth // 4)
                weights.append(
                    pltpu.make_async_copy(
                        w_hbm.at[place, pl.ds(start, half)],
                        w_ref.at[s, place],
                        w_sem.at[4 * s + i],
                    )
                )
        for i in range(blocks):
            copy(k_hbm, k_ref, k_sem, i).start()
            copy(v_hbm, v_ref, v_sem, i).start()
        for weight in weights:
            weight.start()
        for i in range(blocks):
            place = slice(i * step, (i + 1) * step)
            q = q_ref[place].reshape(step, group, size)
            copy(k_hbm, k_ref, k_sem, i).wait()
            scores = lax.dot_general(
                q, k_ref[place], (((2,), (2,)), ((0,), (0,))), preferred_element_type=F32
            )
            scores = scores * scale
            fresh = jnp.sum(
                q.astype(F32) * nk_ref[place].astype(F32)[:, None, :], axis=2, keepdims=True
            )
            fresh = fresh * scale
            position = lax.broadcasted_iota(jnp.int32, (step, group, cache), 2)
            row = lax.broadcasted_iota(jnp.int32, (step, group, cache), 0)
            limit = jnp.full((step, group, cache), len_ref[i * step])
            for j in range(1, step):
                limit = jnp.where(row == j, len_ref[i * step + j], limit)
            scores = jnp.where(position < limit, scores, -jnp.inf)
            top = jnp.maximum(jnp.max(scores, axis=2, keepdims=True), fresh)
            expo = jnp.exp(scores - top)
            expo_new = jnp.exp(fresh - top)
            inverse = 1.0 / (jnp.sum(expo, axis=2, keepdims=True) + expo_new)
            probs = (expo * inverse).astype(BF)
            probs_new = (expo_new * inverse).astype(BF).astype(F32)
            copy(v_hbm, v_ref, v_sem, i).wait()
            result = lax.dot_general(
                probs, v_ref[place], (((2,), (1,)), ((0,), (0,))), preferred_element_type=F32
            )
            result = result + probs_new * nv_ref[place].astype(F32)[:, None, :]
            attn_ref[place, :] = result.reshape(step, depth).astype(BF)
        for weight in weights[:4]:
            weight.wait()
        product = jnp.dot(attn_ref[...], w_ref[0], preferred_element_type=F32)
        theirs_ref[...] = product.astype(BF)
        for weight in weights[4:]:
            weight.wait()
        mine_ref[...] = jnp.dot(attn_ref[...], w_ref[1], preferred_element_type=F32)

    return pl.pallas_call(
        body,
        out_shape=[
            jax.ShapeDtypeStruct((rows, half), BF),
            jax.ShapeDtypeStruct((rows, half), F32),
        ],
        in_specs=[
            pl.BlockSpec(memory_space=pltpu.SMEM),
            pl.BlockSpec(memory_space=pltpu.SMEM),
            pl.BlockSpec(memory_space=pltpu.VMEM),
            pl.BlockSpec(memory_space=pltpu.HBM),
            pl.BlockSpec(memory_space=pltpu.HBM),
            pl.BlockSpec(memory_space=pltpu.VMEM),
            pl.BlockSpec(memory_space=pltpu.VMEM),
            pl.BlockSpec(memory_space=pltpu.HBM),
        ],
        out_specs=whole(2),
        scratch_shapes=[
            pltpu.VMEM((rows, cache, size), BF),
            pltpu.VMEM((rows, cache, size), BF),
            pltpu.VMEM((2, depth, half), BF),
            pltpu.VMEM((rows, depth), BF),
            pltpu.SemaphoreType.DMA((blocks,)),
            pltpu.SemaphoreType.DMA((blocks,)),
            pltpu.SemaphoreType.DMA((8,)),
        ],
        compiler_params=pltpu.CompilerParams(vmem_limit_bytes=57 << 20),
        cost_estimate=pl.CostEstimate(
            flops=0, bytes_accessed=1 << 20, transcendentals=0
        ),
        name="attend",
    )(role.reshape(1), lengths, queries, k_cache, value_cache, new_key, new_value, output_weight)


def of_expert(value, e, per_dev, capacity):
    rows, columns = value.shape
    blocks = rows // (per_dev * capacity)
    return value.reshape(blocks, per_dev, capacity, columns)[:, e].reshape(
        blocks * capacity, columns
    )


def of_all(values, capacity):
    rows, columns = values[0].shape
    blocks = rows // capacity
    parts = [v.reshape(blocks, 1, capacity, columns) for v in values]
    return jnp.concatenate(parts, axis=1).reshape(len(values) * rows, columns)


def experts_act(tokens, gain, w_gate, w_up, capacity):
    roles, slots, half = tokens.shape
    per_dev, width, quarter = w_gate.shape
    chunk = 512

    def body(x_ref, gain_ref, g_any, u_any, act_ref, g_ref, u_ref, sums, sems):
        copies = []
        for k in range(width // chunk):
            rows = pl.ds(k * chunk, chunk)
            copies.append(
                [
                    pltpu.make_async_copy(
                        source.at[:, rows], target.at[:, rows], sems.at[2 * k + i]
                    )
                    for i, (source, target) in enumerate(((g_any, g_ref), (u_any, u_ref)))
                ]
            )
        for pair in copies:
            for copy in pair:
                copy.start()
        square = jnp.zeros((slots, 1), F32)
        for k in range(width // chunk):
            s, place = divmod(k * chunk, half)
            x = x_ref[s, :, place : place + chunk].astype(F32)
            plain = x * (1.0 / gain_ref[s, :, place : place + chunk])
            square = square + jnp.sum(plain * plain, axis=1, keepdims=True)
            for copy in copies[k]:
                copy.wait()
            for e in range(per_dev):
                one = of_expert(x, e, per_dev, capacity).astype(BF)
                for i, w_ref in enumerate((g_ref, u_ref)):
                    product = jnp.dot(
                        one, w_ref[e, k * chunk : (k + 1) * chunk], preferred_element_type=F32
                    )
                    if k:
                        product = product + sums[2 * e + i]
                    sums[2 * e + i] = product
        inverse = lax.rsqrt(square / width + EPS)
        gate = of_all([sums[2 * e] for e in range(per_dev)], capacity) * inverse
        upper = of_all([sums[2 * e + 1] for e in range(per_dev)], capacity) * inverse
        act_ref[...] = (gate / (1.0 + jnp.exp(-gate)) * upper).astype(BF)

    return pl.pallas_call(
        body,
        out_shape=jax.ShapeDtypeStruct((slots, quarter), BF),
        in_specs=whole(2) + [pl.BlockSpec(memory_space=pl.ANY)] * 2,
        out_specs=pl.BlockSpec(memory_space=pltpu.VMEM),
        scratch_shapes=[
            pltpu.VMEM(w_gate.shape, BF),
            pltpu.VMEM(w_up.shape, BF),
            pltpu.VMEM((2 * per_dev, slots // per_dev, quarter), F32),
            pltpu.SemaphoreType.DMA((2 * (width // chunk),)),
        ],
        compiler_params=pltpu.CompilerParams(vmem_limit_bytes=57 << 20),
        cost_estimate=pl.CostEstimate(
            flops=4 * slots * width * quarter, bytes_accessed=10 << 20, transcendentals=0
        ),
        name="experts_act",
    )(tokens, gain, w_gate, w_up)


def far_down(act, downs, capacity):
    slots, _ = act.shape
    per_dev = len(downs)
    columns = downs[0].shape[1]

    def body(a_ref, *refs):
        w_refs, out_ref = refs[:-1], refs[-1]
        value = a_ref[...].astype(F32)
        products = [
            jnp.dot(
                of_expert(value, e, per_dev, capacity).astype(BF),
                w_ref[...],
                preferred_element_type=F32,
            )
            for e, w_ref in enumerate(w_refs)
        ]
        out_ref[...] = of_all(products, capacity).astype(BF)

    return pl.pallas_call(
        body,
        out_shape=jax.ShapeDtypeStruct((slots, columns), BF),
        in_specs=whole(1 + per_dev),
        out_specs=pl.BlockSpec(memory_space=pltpu.VMEM),
        compiler_params=pltpu.CompilerParams(vmem_limit_bytes=24 << 20),
        name="far_down",
    )(act, *downs)


def experts_down(acts, downs, far, capacity, roles):
    count = len(acts)
    slots, quarter = acts[0].shape
    per_dev = len(downs[0])
    columns = downs[0][0].shape[1]
    piece = columns // roles

    def body(*refs):
        a_refs, w_refs, (far_ref, out_ref) = refs[:count], refs[count:-2], refs[-2:]
        ones = [
            [of_expert(a[...].astype(F32), e, per_dev, capacity).astype(BF) for e in range(per_dev)]
            for a in a_refs
        ]
        for s in range(roles):
            totals = []
            for e in range(per_dev):
                total = None
                for i in range(count):
                    product = jnp.dot(
                        ones[i][e],
                        w_refs[i * per_dev + e][:, s * piece : (s + 1) * piece],
                        preferred_element_type=F32,
                    )
                    total = product if total is None else total + product
                totals.append(total)
            total = of_all(totals, capacity) + far_ref[:, s * piece : (s + 1) * piece].astype(F32)
            out_ref[s * slots : (s + 1) * slots] = total.astype(BF)

    flat = [w for each in downs for w in each]
    return pl.pallas_call(
        body,
        out_shape=jax.ShapeDtypeStruct((roles * slots, piece), BF),
        in_specs=whole(count + len(flat) + 1),
        out_specs=pl.BlockSpec(memory_space=pltpu.VMEM),
        compiler_params=pltpu.CompilerParams(vmem_limit_bytes=24 << 20),
        cost_estimate=pl.CostEstimate(
            flops=2 * slots * count * quarter * columns, bytes_accessed=5 << 20, transcendentals=0
        ),
        name="experts_down",
    )(*acts, *flat, far)


def per_device(
    queries,
    k_cache,
    value_cache,
    new_token_key,
    new_token_value,
    lengths,
    output_weight,
    residual,
    norm_gain,
    routes,
    route_scores,
    w_gate,
    w_up,
    w_down,
):
    rows_here = queries.shape[0]
    width = residual.shape[1]
    roles = lax.axis_size("role")
    heads_count = lax.axis_size("heads")
    shards = lax.axis_size("rows")
    half = width // roles
    piece = half // heads_count
    per_dev, _, quarter = w_gate.shape
    experts = per_dev * shards * roles
    capacity = 8
    role = lax.axis_index("role")
    head = lax.axis_index("heads")
    swap = [(i, roles - 1 - i) for i in range(roles)]

    def shift(x, step):
        return lax.ppermute(
            x, "heads", [(i, (i + step) % heads_count) for i in range(heads_count)]
        )

    theirs, mine = attend(
        queries[:, 0, 0],
        k_cache[:, 0],
        value_cache[:, 0],
        new_token_key[:, 0],
        new_token_value[:, 0],
        lengths,
        output_weight[0, 0],
        role,
    )
    received = lax.ppermute(theirs, "role", swap)
    chip = (mine + received.astype(F32)).astype(BF)
    chip, w_down = lax.optimization_barrier((chip, w_down))
    across, near = heads_count // 2, (0, 1, heads_count - 1)
    pieces = [(step, e) for step in (*near, across) for e in range(per_dev)]
    rest = cut_down(w_down, head, heads_count, roles, pieces)
    total = chip.astype(F32)
    for step in range(1, heads_count):
        total = total + shift(chip, step).astype(F32)
    first = role == 0
    resid = jnp.where(first, residual[:, :half], residual[:, half:]).astype(F32)
    gain = jnp.where(first, norm_gain[:half], norm_gain[half:])
    hidden = resid + total
    hidden, *rest = lax.optimization_barrier((hidden, *rest))
    downs = [
        [shift(part, step) if step else part for part in rest[i * per_dev : (i + 1) * per_dev]]
        for i, step in enumerate(near)
    ]
    scaled = (hidden * gain).astype(BF)

    named = routes[:, :, None] == jnp.arange(experts, dtype=jnp.int32)
    chosen = jnp.any(named, axis=1)
    shares = route_scores / jnp.sum(route_scores, axis=1, keepdims=True)
    coef = jnp.sum(jnp.where(named, shares[:, :, None], F32(0.0)), axis=1)
    order = jnp.arange(rows_here, dtype=jnp.int32)
    before = (order[None, :] < order[:, None]).astype(BF)
    rank = jnp.dot(before, chosen.astype(BF), preferred_element_type=F32).astype(jnp.int32)
    taken = chosen[:, :, None] & (rank[:, :, None] == jnp.arange(capacity, dtype=jnp.int32))
    slots = experts * capacity
    pick = taken.reshape(rows_here, slots).astype(BF)
    mixing = jnp.where(taken, coef[:, :, None], F32(0.0)).reshape(rows_here, slots)

    outgoing = lax.dot_general(
        pick, scaled, (((0,), (0,)), ((), ())), preferred_element_type=F32
    ).astype(BF)
    outgoing = outgoing.reshape(roles * shards, per_dev * capacity, half)
    incoming = lax.all_to_all(outgoing, ("role", "rows"), 0, 0, tiled=True)
    tokens = incoming.reshape(roles, shards * per_dev * capacity, half)
    act = experts_act(tokens, norm_gain.reshape(roles, 1, half), w_gate, w_up, capacity)
    far = shift(far_down(act, rest[len(near) * per_dev :], capacity), across)
    acts = [shift(act, step) if step else act for step in near]
    result = experts_down(acts, downs, far, capacity, roles)
    result = result.reshape(roles * shards, per_dev * capacity, piece)
    returned = lax.all_to_all(result, ("role", "rows"), 0, 0, tiled=True)
    returned = returned.reshape(slots, piece)
    mix_high = mixing.astype(BF)
    mix_low = (mixing - mix_high.astype(F32)).astype(BF)
    moe = jnp.dot(mix_high, returned, preferred_element_type=F32) + jnp.dot(
        mix_low, returned, preferred_element_type=F32
    )
    own = lax.dynamic_slice_in_dim(hidden, head * piece, piece, 1)
    return (own + moe).astype(BF)


def solution(mesh):
    in_specs = (
        P("rows", "role", "heads", None),
        P("rows", "heads", None, None),
        P("rows", "heads", None, None),
        P("rows", "heads", None),
        P("rows", "heads", None),
        P("rows"),
        P("role", "heads", None, None),
        P("rows", None),
        P(),
        P("rows", None),
        P("rows", None),
        P(("role", "rows"), None, "heads"),
        P(("role", "rows"), None, "heads"),
        P(("role", "rows"), "heads", None),
    )
    out_specs = P("rows", ("role", "heads"))
    return jax.shard_map(
        per_device, mesh=mesh, in_specs=in_specs, out_specs=out_specs, check_vma=False
    )
```

```python
import math

import jax
import jax.numpy as jnp
from jax import lax
from jax.experimental import pallas as pl
from jax.experimental.pallas import tpu as pltpu
from jax.sharding import PartitionSpec as P

BF = jnp.bfloat16
F32 = jnp.float32
EPS = 1e-06
VMEM = 60 << 20


def whole(n):
    return [pl.BlockSpec(memory_space=pltpu.VMEM)] * n


def cut_down(w_down, head, heads_count, roles, pieces):
    per_dev, quarter, width = w_down.shape
    half = width // roles
    piece = half // heads_count
    parts = 4
    count = len(pieces)

    def body(head_ref, w_hbm, *rest):
        outs, w_ref, in_sems, out_sems = rest[:count], *rest[count:]
        loads, stores = [], []
        for e in range(per_dev):
            for i in range(parts):
                rows = pl.ds(i * (quarter // parts), quarter // parts)
                loads.append(
                    pltpu.make_async_copy(
                        w_hbm.at[e, rows], w_ref.at[e, rows], in_sems.at[e * parts + i]
                    )
                )
        for i, (step, e) in enumerate(pieces):
            place = lax.rem(head_ref[0] + step, heads_count)
            for s in range(roles):
                start = pl.multiple_of(s * half + place * piece, piece)
                stores.append(
                    pltpu.make_async_copy(
                        w_ref.at[e, :, pl.ds(start, piece)],
                        outs[i].at[:, pl.ds(s * piece, piece)],
                        out_sems.at[i * roles + s],
                    )
                )
        for load in loads:
            load.start()
        for e in range(per_dev):
            for load in loads[e * parts : (e + 1) * parts]:
                load.wait()
            for i, (_, mine) in enumerate(pieces):
                if mine == e:
                    for store in stores[i * roles : (i + 1) * roles]:
                        store.start()
        for store in stores:
            store.wait()

    return pl.pallas_call(
        body,
        out_shape=[jax.ShapeDtypeStruct((quarter, roles * piece), BF)] * count,
        in_specs=[pl.BlockSpec(memory_space=pltpu.SMEM), pl.BlockSpec(memory_space=pltpu.HBM)],
        out_specs=[pl.BlockSpec(memory_space=pltpu.HBM)] * count,
        scratch_shapes=[
            pltpu.VMEM(w_down.shape, BF),
            pltpu.SemaphoreType.DMA((per_dev * parts,)),
            pltpu.SemaphoreType.DMA((count * roles,)),
        ],
        compiler_params=pltpu.CompilerParams(vmem_limit_bytes=VMEM),
        cost_estimate=pl.CostEstimate(
            flops=0, bytes_accessed=2 * w_down.size * 2, transcendentals=0
        ),
        name="cut_down",
    )(head.reshape(1), w_down)


def attend(queries, k_cache, value_cache, new_key, new_value, lengths, output_weight, role):
    rows, depth = queries.shape
    cache, size = k_cache.shape[1:]
    group = depth // size
    width = output_weight.shape[1]
    half = width // 2
    step = 16
    blocks = rows // step
    scale = 1.0 / math.sqrt(size)

    def body(
        role_ref, len_ref, q_ref, k_hbm, v_hbm, nk_ref, nv_ref, w_hbm,
        theirs_ref, mine_ref, k_ref, v_ref, w_ref, attn_ref, k_sem, v_sem, w_sem,
    ):
        def copy(hbm, ref, sem, i):
            place = pl.ds(i * step, step)
            return pltpu.make_async_copy(hbm.at[place], ref.at[place], sem.at[i])

        weights = []
        for s in range(2):
            side = role_ref[0] if s else 1 - role_ref[0]
            start = pl.multiple_of(side * half, half)
            for i in range(4):
                place = pl.ds(i * (depth // 4), depth // 4)
                weights.append(
                    pltpu.make_async_copy(
                        w_hbm.at[place, pl.ds(start, half)],
                        w_ref.at[s, place],
                        w_sem.at[4 * s + i],
                    )
                )
        for i in range(blocks):
            copy(k_hbm, k_ref, k_sem, i).start()
            copy(v_hbm, v_ref, v_sem, i).start()
        for i in range(blocks):
            place = slice(i * step, (i + 1) * step)
            q = q_ref[place].reshape(step, group, size)
            copy(k_hbm, k_ref, k_sem, i).wait()
            if i == 0:
                for weight in weights:
                    weight.start()
            scores = lax.dot_general(
                q, k_ref[place], (((2,), (2,)), ((0,), (0,))), preferred_element_type=F32
            )
            scores = scores * scale
            fresh = jnp.sum(
                q.astype(F32) * nk_ref[place].astype(F32)[:, None, :], axis=2, keepdims=True
            )
            fresh = fresh * scale
            position = lax.broadcasted_iota(jnp.int32, (step, group, cache), 2)
            row = lax.broadcasted_iota(jnp.int32, (step, group, cache), 0)
            limit = jnp.full((step, group, cache), len_ref[i * step])
            for j in range(1, step):
                limit = jnp.where(row == j, len_ref[i * step + j], limit)
            scores = jnp.where(position < limit, scores, -jnp.inf)
            top = jnp.maximum(jnp.max(scores, axis=2, keepdims=True), fresh)
            expo = jnp.exp(scores - top)
            expo_new = jnp.exp(fresh - top)
            inverse = 1.0 / (jnp.sum(expo, axis=2, keepdims=True) + expo_new)
            probs = (expo * inverse).astype(BF)
            probs_new = (expo_new * inverse).astype(BF).astype(F32)
            copy(v_hbm, v_ref, v_sem, i).wait()
            result = lax.dot_general(
                probs, v_ref[place], (((2,), (1,)), ((0,), (0,))), preferred_element_type=F32
            )
            result = result + probs_new * nv_ref[place].astype(F32)[:, None, :]
            attn_ref[place, :] = result.reshape(step, depth).astype(BF)
        for weight in weights[:4]:
            weight.wait()
        product = jnp.dot(attn_ref[...], w_ref[0], preferred_element_type=F32)
        theirs_ref[...] = product.astype(BF)
        for weight in weights[4:]:
            weight.wait()
        mine_ref[...] = jnp.dot(attn_ref[...], w_ref[1], preferred_element_type=F32)

    return pl.pallas_call(
        body,
        out_shape=[
            jax.ShapeDtypeStruct((rows, half), BF),
            jax.ShapeDtypeStruct((rows, half), F32),
        ],
        in_specs=[
            pl.BlockSpec(memory_space=pltpu.SMEM),
            pl.BlockSpec(memory_space=pltpu.SMEM),
            pl.BlockSpec(memory_space=pltpu.VMEM),
            pl.BlockSpec(memory_space=pltpu.HBM),
            pl.BlockSpec(memory_space=pltpu.HBM),
            pl.BlockSpec(memory_space=pltpu.VMEM),
            pl.BlockSpec(memory_space=pltpu.VMEM),
            pl.BlockSpec(memory_space=pltpu.HBM),
        ],
        out_specs=whole(2),
        scratch_shapes=[
            pltpu.VMEM((rows, cache, size), BF),
            pltpu.VMEM((rows, cache, size), BF),
            pltpu.VMEM((2, depth, half), BF),
            pltpu.VMEM((rows, depth), BF),
            pltpu.SemaphoreType.DMA((blocks,)),
            pltpu.SemaphoreType.DMA((blocks,)),
            pltpu.SemaphoreType.DMA((8,)),
        ],
        compiler_params=pltpu.CompilerParams(vmem_limit_bytes=57 << 20),
        cost_estimate=pl.CostEstimate(
            flops=0, bytes_accessed=1 << 20, transcendentals=0
        ),
        name="attend",
    )(role.reshape(1), lengths, queries, k_cache, value_cache, new_key, new_value, output_weight)


def of_expert(value, e, per_dev, capacity):
    rows, columns = value.shape
    blocks = rows // (per_dev * capacity)
    return value.reshape(blocks, per_dev, capacity, columns)[:, e].reshape(
        blocks * capacity, columns
    )


def of_all(values, capacity):
    rows, columns = values[0].shape
    blocks = rows // capacity
    parts = [v.reshape(blocks, 1, capacity, columns) for v in values]
    return jnp.concatenate(parts, axis=1).reshape(len(values) * rows, columns)


def expert_act(tokens, gain, w_gate, w_up, across, e, before, capacity):
    roles, slots, half = tokens.shape
    per_dev, width, quarter = w_gate.shape
    columns = across.shape[1]
    chunk = 512
    rows = slots // per_dev
    done = e * rows

    def body(x_ref, gain_ref, g_hbm, u_hbm, w_ref, *rest):
        before_ref = rest[0] if e else None
        act_ref, far_ref, g_ref, u_ref, sums, sems = rest[1 if e else 0 :]
        copies = []
        for k in range(width // chunk):
            place = pl.ds(k * chunk, chunk)
            copies.append(
                [
                    pltpu.make_async_copy(hbm.at[e, place], ref.at[place], sems.at[2 * k + i])
                    for i, (hbm, ref) in enumerate(((g_hbm, g_ref), (u_hbm, u_ref)))
                ]
            )
        for pair in copies:
            for copy in pair:
                copy.start()
        square = jnp.zeros((rows, 1), F32)
        for k in range(width // chunk):
            s, place = divmod(k * chunk, half)
            x = x_ref[s, :, place : place + chunk].astype(F32)
            x = of_expert(x, e, per_dev, capacity)
            plain = x * (1.0 / gain_ref[s, :, place : place + chunk])
            square = square + jnp.sum(plain * plain, axis=1, keepdims=True)
            x = x.astype(BF)
            for copy in copies[k]:
                copy.wait()
            for i, ref in enumerate((g_ref, u_ref)):
                product = jnp.dot(
                    x, ref[k * chunk : (k + 1) * chunk], preferred_element_type=F32
                )
                sums[i] = product + sums[i] if k else product
        inverse = lax.rsqrt(square / width + EPS)
        gate, upper = sums[0] * inverse, sums[1] * inverse
        act = (gate / (1.0 + jnp.exp(-gate)) * upper).astype(BF)
        if e:
            act_ref[:done] = before_ref[...]
        act_ref[done:] = act
        far_ref[...] = jnp.dot(act, w_ref[...], preferred_element_type=F32).astype(BF)

    return pl.pallas_call(
        body,
        out_shape=[
            jax.ShapeDtypeStruct((done + rows, quarter), BF),
            jax.ShapeDtypeStruct((rows, columns), BF),
        ],
        in_specs=whole(2)
        + [pl.BlockSpec(memory_space=pltpu.HBM)] * 2
        + whole(2 if e else 1),
        out_specs=whole(2),
        scratch_shapes=[
            pltpu.VMEM((width, quarter), BF),
            pltpu.VMEM((width, quarter), BF),
            pltpu.VMEM((2, rows, quarter), F32),
            pltpu.SemaphoreType.DMA((2 * (width // chunk),)),
        ],
        compiler_params=pltpu.CompilerParams(vmem_limit_bytes=57 << 20),
        cost_estimate=pl.CostEstimate(
            flops=4 * rows * width * quarter, bytes_accessed=6 << 20, transcendentals=0
        ),
        name=f"expert_act_{e}",
    )(tokens, gain, w_gate, w_up, across, *([before] if e else []))


def experts_down(acts, downs, fars, capacity, roles):
    count = len(acts)
    slots, quarter = acts[0].shape
    per_dev = len(fars)
    rows, columns = fars[0].shape
    piece = columns // roles

    def body(*refs):
        a_refs, w_refs = refs[:count], refs[count : count + count * per_dev]
        far_refs, out_ref = refs[count + count * per_dev : -1], refs[-1]
        for s in range(roles):
            totals = []
            for e in range(per_dev):
                total = far_refs[e][:, s * piece : (s + 1) * piece].astype(F32)
                for i in range(count):
                    total = total + jnp.dot(
                        a_refs[i][e * rows : (e + 1) * rows],
                        w_refs[i * per_dev + e][:, s * piece : (s + 1) * piece],
                        preferred_element_type=F32,
                    )
                totals.append(total)
            out_ref[s * slots : (s + 1) * slots] = of_all(totals, capacity).astype(BF)

    flat = [w for each in downs for w in each]
    return pl.pallas_call(
        body,
        out_shape=jax.ShapeDtypeStruct((roles * slots, piece), BF),
        in_specs=whole(count + len(flat) + per_dev),
        out_specs=pl.BlockSpec(memory_space=pltpu.VMEM),
        compiler_params=pltpu.CompilerParams(vmem_limit_bytes=24 << 20),
        cost_estimate=pl.CostEstimate(
            flops=2 * slots * count * quarter * columns, bytes_accessed=5 << 20, transcendentals=0
        ),
        name="experts_down",
    )(*acts, *flat, *fars)


def choose(parts, residual, gain, pick):
    rows, half = residual.shape
    slots = pick.shape[0]
    count = len(parts)
    steps = 4
    block = slots // steps

    def body(*refs):
        part_refs = refs[:count]
        resid_ref, gain_ref, pick_ref, hidden_ref, out_ref, scaled_ref = refs[count:]

        @pl.when(pl.program_id(0) == 0)
        def _():
            hidden = resid_ref[...].astype(F32)
            for ref in part_refs:
                hidden = hidden + ref[...].astype(F32)
            hidden_ref[...] = hidden
            scaled_ref[...] = (hidden * gain_ref[...]).astype(BF)

        out_ref[...] = jnp.dot(
            pick_ref[...], scaled_ref[...], preferred_element_type=F32
        ).astype(BF)

    fixed = pl.BlockSpec((rows, half), lambda i: (0, 0))
    return pl.pallas_call(
        body,
        grid=(steps,),
        out_shape=[
            jax.ShapeDtypeStruct((rows, half), F32),
            jax.ShapeDtypeStruct((slots, half), BF),
        ],
        in_specs=[fixed] * (count + 1)
        + [
            pl.BlockSpec((1, half), lambda i: (0, 0)),
            pl.BlockSpec((block, rows), lambda i: (i, 0)),
        ],
        out_specs=[fixed, pl.BlockSpec((block, half), lambda i: (i, 0))],
        scratch_shapes=[pltpu.VMEM((rows, half), BF)],
        compiler_params=pltpu.CompilerParams(vmem_limit_bytes=24 << 20),
        name="choose",
    )(*parts, residual, gain, pick)


def per_device(
    queries,
    k_cache,
    value_cache,
    new_token_key,
    new_token_value,
    lengths,
    output_weight,
    residual,
    norm_gain,
    routes,
    route_scores,
    w_gate,
    w_up,
    w_down,
):
    rows_here = queries.shape[0]
    width = residual.shape[1]
    roles = lax.axis_size("role")
    heads_count = lax.axis_size("heads")
    shards = lax.axis_size("rows")
    half = width // roles
    piece = half // heads_count
    per_dev, _, quarter = w_gate.shape
    experts = per_dev * shards * roles
    capacity = 8
    role = lax.axis_index("role")
    head = lax.axis_index("heads")
    swap = [(i, roles - 1 - i) for i in range(roles)]

    def shift(x, step):
        return lax.ppermute(
            x, "heads", [(i, (i + step) % heads_count) for i in range(heads_count)]
        )

    theirs, mine = attend(
        queries[:, 0, 0],
        k_cache[:, 0],
        value_cache[:, 0],
        new_token_key[:, 0],
        new_token_value[:, 0],
        lengths,
        output_weight[0, 0],
        role,
    )
    received = lax.ppermute(theirs, "role", swap)
    chip = (mine + received.astype(F32)).astype(BF)
    chip, w_down = lax.optimization_barrier((chip, w_down))
    across, near = heads_count // 2, (0, 1, heads_count - 1)
    pieces = [(step, e) for step in (*near, across) for e in range(per_dev)]
    rest = cut_down(w_down, head, heads_count, roles, pieces)

    named = routes[:, :, None] == jnp.arange(experts, dtype=jnp.int32)
    chosen = jnp.any(named, axis=1)
    shares = route_scores / jnp.sum(route_scores, axis=1, keepdims=True)
    coef = jnp.sum(jnp.where(named, shares[:, :, None], F32(0.0)), axis=1)
    order = jnp.arange(rows_here, dtype=jnp.int32)
    before = (order[None, :] < order[:, None]).astype(BF)
    rank = jnp.dot(before, chosen.astype(BF), preferred_element_type=F32).astype(jnp.int32)
    taken = chosen[:, :, None] & (rank[:, :, None] == jnp.arange(capacity, dtype=jnp.int32))
    slots = experts * capacity
    pick = taken.reshape(rows_here, slots).T.astype(BF)
    mixing = jnp.where(taken, coef[:, :, None], F32(0.0)).reshape(rows_here, slots)

    parts = [shift(chip, step) if step else chip for step in range(heads_count)]
    first = role == 0
    resid = jnp.where(first, residual[:, :half], residual[:, half:])
    gain = jnp.where(first, norm_gain[:half], norm_gain[half:]).reshape(1, half)
    parts[0], *rest = lax.optimization_barrier((parts[0], *rest))
    hidden, outgoing = choose(parts, resid, gain, pick)
    hidden, *rest = lax.optimization_barrier((hidden, *rest))
    downs = [
        [shift(part, step) if step else part for part in rest[i * per_dev : (i + 1) * per_dev]]
        for i, step in enumerate(near)
    ]
    outgoing = outgoing.reshape(roles * shards, per_dev * capacity, half)
    incoming = lax.all_to_all(outgoing, ("role", "rows"), 0, 0, tiled=True)
    tokens = incoming.reshape(roles, shards * per_dev * capacity, half)
    flat_gain = norm_gain.reshape(roles, 1, half)
    act, fars = None, []
    for e in range(per_dev):
        opposite = rest[len(near) * per_dev + e]
        act, far = expert_act(tokens, flat_gain, w_gate, w_up, opposite, e, act, capacity)
        fars.append(shift(far, across))
    acts = [shift(act, step) if step else act for step in near]
    result = experts_down(acts, downs, fars, capacity, roles)
    result = result.reshape(roles * shards, per_dev * capacity, piece)
    returned = lax.all_to_all(result, ("role", "rows"), 0, 0, tiled=True)
    returned = returned.reshape(slots, piece)
    mix_high = mixing.astype(BF)
    mix_low = (mixing - mix_high.astype(F32)).astype(BF)
    moe = jnp.dot(mix_high, returned, preferred_element_type=F32) + jnp.dot(
        mix_low, returned, preferred_element_type=F32
    )
    own = lax.dynamic_slice_in_dim(hidden, head * piece, piece, 1)
    return (own + moe).astype(BF)


def solution(mesh):
    in_specs = (
        P("rows", "role", "heads", None),
        P("rows", "heads", None, None),
        P("rows", "heads", None, None),
        P("rows", "heads", None),
        P("rows", "heads", None),
        P("rows"),
        P("role", "heads", None, None),
        P("rows", None),
        P(),
        P("rows", None),
        P("rows", None),
        P(("role", "rows"), None, "heads"),
        P(("role", "rows"), None, "heads"),
        P(("role", "rows"), "heads", None),
    )
    out_specs = P("rows", ("role", "heads"))
    return jax.shard_map(
        per_device, mesh=mesh, in_specs=in_specs, out_specs=out_specs, check_vma=False
    )
```

```python
import math

import jax
import jax.numpy as jnp
from jax import lax
from jax.experimental import pallas as pl
from jax.experimental.pallas import tpu as pltpu
from jax.sharding import PartitionSpec as P

BF = jnp.bfloat16
F32 = jnp.float32
EPS = 1e-06
VMEM = 60 << 20


def whole(n):
    return [pl.BlockSpec(memory_space=pltpu.VMEM)] * n


def cut_down(w_down, head, heads_count, roles, pieces):
    per_dev, quarter, width = w_down.shape
    half = width // roles
    piece = half // heads_count
    parts = 4
    count = len(pieces)

    def body(head_ref, w_hbm, *rest):
        outs, w_ref, in_sems, out_sems = rest[:count], *rest[count:]
        loads, stores = [], []
        for e in range(per_dev):
            for i in range(parts):
                rows = pl.ds(i * (quarter // parts), quarter // parts)
                loads.append(
                    pltpu.make_async_copy(
                        w_hbm.at[e, rows], w_ref.at[e, rows], in_sems.at[e * parts + i]
                    )
                )
        for i, (step, e) in enumerate(pieces):
            place = lax.rem(head_ref[0] + step, heads_count)
            for s in range(roles):
                start = pl.multiple_of(s * half + place * piece, piece)
                stores.append(
                    pltpu.make_async_copy(
                        w_ref.at[e, :, pl.ds(start, piece)],
                        outs[i].at[:, pl.ds(s * piece, piece)],
                        out_sems.at[i * roles + s],
                    )
                )
        for load in loads:
            load.start()
        for e in range(per_dev):
            for load in loads[e * parts : (e + 1) * parts]:
                load.wait()
            for i, (_, mine) in enumerate(pieces):
                if mine == e:
                    for store in stores[i * roles : (i + 1) * roles]:
                        store.start()
        for store in stores:
            store.wait()

    return pl.pallas_call(
        body,
        out_shape=[jax.ShapeDtypeStruct((quarter, roles * piece), BF)] * count,
        in_specs=[pl.BlockSpec(memory_space=pltpu.SMEM), pl.BlockSpec(memory_space=pltpu.HBM)],
        out_specs=[pl.BlockSpec(memory_space=pltpu.HBM)] * count,
        scratch_shapes=[
            pltpu.VMEM(w_down.shape, BF),
            pltpu.SemaphoreType.DMA((per_dev * parts,)),
            pltpu.SemaphoreType.DMA((count * roles,)),
        ],
        compiler_params=pltpu.CompilerParams(vmem_limit_bytes=VMEM),
        cost_estimate=pl.CostEstimate(
            flops=0, bytes_accessed=2 * w_down.size * 2, transcendentals=0
        ),
        name="cut_down",
    )(head.reshape(1), w_down)


def attend(queries, k_cache, value_cache, new_key, new_value, lengths, output_weight, role):
    rows, depth = queries.shape
    cache, size = k_cache.shape[1:]
    group = depth // size
    width = output_weight.shape[1]
    half = width // 2
    step = 16
    blocks = rows // step
    scale = 1.0 / math.sqrt(size)

    def body(
        role_ref, len_ref, q_ref, k_hbm, v_hbm, nk_ref, nv_ref, w_hbm,
        theirs_ref, mine_ref, k_ref, v_ref, w_ref, attn_ref, k_sem, v_sem, w_sem,
    ):
        def copy(hbm, ref, sem, i):
            place = pl.ds(i * step, step)
            return pltpu.make_async_copy(hbm.at[place], ref.at[place], sem.at[i])

        weights = []
        for s in range(2):
            side = role_ref[0] if s else 1 - role_ref[0]
            start = pl.multiple_of(side * half, half)
            for i in range(4):
                place = pl.ds(i * (depth // 4), depth // 4)
                weights.append(
                    pltpu.make_async_copy(
                        w_hbm.at[place, pl.ds(start, half)],
                        w_ref.at[s, place],
                        w_sem.at[4 * s + i],
                    )
                )
        for i in range(blocks):
            copy(k_hbm, k_ref, k_sem, i).start()
            copy(v_hbm, v_ref, v_sem, i).start()
        for i in range(blocks):
            place = slice(i * step, (i + 1) * step)
            q = q_ref[place].reshape(step, group, size)
            copy(k_hbm, k_ref, k_sem, i).wait()
            if i == 0:
                for weight in weights:
                    weight.start()
            scores = lax.dot_general(
                q, k_ref[place], (((2,), (2,)), ((0,), (0,))), preferred_element_type=F32
            )
            scores = scores * scale
            fresh = jnp.sum(
                q.astype(F32) * nk_ref[place].astype(F32)[:, None, :], axis=2, keepdims=True
            )
            fresh = fresh * scale
            position = lax.broadcasted_iota(jnp.int32, (step, group, cache), 2)
            row = lax.broadcasted_iota(jnp.int32, (step, group, cache), 0)
            limit = jnp.full((step, group, cache), len_ref[i * step])
            for j in range(1, step):
                limit = jnp.where(row == j, len_ref[i * step + j], limit)
            scores = jnp.where(position < limit, scores, -jnp.inf)
            top = jnp.maximum(jnp.max(scores, axis=2, keepdims=True), fresh)
            expo = jnp.exp(scores - top)
            expo_new = jnp.exp(fresh - top)
            inverse = 1.0 / (jnp.sum(expo, axis=2, keepdims=True) + expo_new)
            probs = (expo * inverse).astype(BF)
            probs_new = (expo_new * inverse).astype(BF).astype(F32)
            copy(v_hbm, v_ref, v_sem, i).wait()
            result = lax.dot_general(
                probs, v_ref[place], (((2,), (1,)), ((0,), (0,))), preferred_element_type=F32
            )
            result = result + probs_new * nv_ref[place].astype(F32)[:, None, :]
            attn_ref[place, :] = result.reshape(step, depth).astype(BF)
        for weight in weights[:4]:
            weight.wait()
        product = jnp.dot(attn_ref[...], w_ref[0], preferred_element_type=F32)
        theirs_ref[...] = product.astype(BF)
        for weight in weights[4:]:
            weight.wait()
        mine_ref[...] = jnp.dot(attn_ref[...], w_ref[1], preferred_element_type=F32)

    return pl.pallas_call(
        body,
        out_shape=[
            jax.ShapeDtypeStruct((rows, half), BF),
            jax.ShapeDtypeStruct((rows, half), F32),
        ],
        in_specs=[
            pl.BlockSpec(memory_space=pltpu.SMEM),
            pl.BlockSpec(memory_space=pltpu.SMEM),
            pl.BlockSpec(memory_space=pltpu.VMEM),
            pl.BlockSpec(memory_space=pltpu.HBM),
            pl.BlockSpec(memory_space=pltpu.HBM),
            pl.BlockSpec(memory_space=pltpu.VMEM),
            pl.BlockSpec(memory_space=pltpu.VMEM),
            pl.BlockSpec(memory_space=pltpu.HBM),
        ],
        out_specs=whole(2),
        scratch_shapes=[
            pltpu.VMEM((rows, cache, size), BF),
            pltpu.VMEM((rows, cache, size), BF),
            pltpu.VMEM((2, depth, half), BF),
            pltpu.VMEM((rows, depth), BF),
            pltpu.SemaphoreType.DMA((blocks,)),
            pltpu.SemaphoreType.DMA((blocks,)),
            pltpu.SemaphoreType.DMA((8,)),
        ],
        compiler_params=pltpu.CompilerParams(vmem_limit_bytes=57 << 20),
        cost_estimate=pl.CostEstimate(
            flops=0, bytes_accessed=1 << 20, transcendentals=0
        ),
        name="attend",
    )(role.reshape(1), lengths, queries, k_cache, value_cache, new_key, new_value, output_weight)


def of_expert(value, e, per_dev, capacity):
    rows, columns = value.shape
    blocks = rows // (per_dev * capacity)
    return value.reshape(blocks, per_dev, capacity, columns)[:, e].reshape(
        blocks * capacity, columns
    )


def of_all(values, capacity):
    rows, columns = values[0].shape
    blocks = rows // capacity
    parts = [v.reshape(blocks, 1, capacity, columns) for v in values]
    return jnp.concatenate(parts, axis=1).reshape(len(values) * rows, columns)


def experts_act(tokens, gain, w_gate, w_up, capacity):
    roles, slots, half = tokens.shape
    per_dev, width, quarter = w_gate.shape
    chunk = 512

    def body(x_ref, gain_ref, g_any, u_any, act_ref, g_ref, u_ref, sums, sems):
        copies = []
        for k in range(width // chunk):
            rows = pl.ds(k * chunk, chunk)
            copies.append(
                [
                    pltpu.make_async_copy(
                        source.at[:, rows], target.at[:, rows], sems.at[2 * k + i]
                    )
                    for i, (source, target) in enumerate(((g_any, g_ref), (u_any, u_ref)))
                ]
            )
        for pair in copies:
            for copy in pair:
                copy.start()
        square = jnp.zeros((slots, 1), F32)
        for k in range(width // chunk):
            s, place = divmod(k * chunk, half)
            x = x_ref[s, :, place : place + chunk].astype(F32)
            plain = x * (1.0 / gain_ref[s, :, place : place + chunk])
            square = square + jnp.sum(plain * plain, axis=1, keepdims=True)
            for copy in copies[k]:
                copy.wait()
            for e in range(per_dev):
                one = of_expert(x, e, per_dev, capacity).astype(BF)
                for i, w_ref in enumerate((g_ref, u_ref)):
                    product = jnp.dot(
                        one, w_ref[e, k * chunk : (k + 1) * chunk], preferred_element_type=F32
                    )
                    if k:
                        product = product + sums[2 * e + i]
                    sums[2 * e + i] = product
        inverse = lax.rsqrt(square / width + EPS)
        gate = of_all([sums[2 * e] for e in range(per_dev)], capacity) * inverse
        upper = of_all([sums[2 * e + 1] for e in range(per_dev)], capacity) * inverse
        act_ref[...] = (gate / (1.0 + jnp.exp(-gate)) * upper).astype(BF)

    return pl.pallas_call(
        body,
        out_shape=jax.ShapeDtypeStruct((slots, quarter), BF),
        in_specs=whole(2) + [pl.BlockSpec(memory_space=pltpu.HBM)] * 2,
        out_specs=pl.BlockSpec(memory_space=pltpu.VMEM),
        scratch_shapes=[
            pltpu.VMEM(w_gate.shape, BF),
            pltpu.VMEM(w_up.shape, BF),
            pltpu.VMEM((2 * per_dev, slots // per_dev, quarter), F32),
            pltpu.SemaphoreType.DMA((2 * (width // chunk),)),
        ],
        compiler_params=pltpu.CompilerParams(vmem_limit_bytes=49 << 20),
        cost_estimate=pl.CostEstimate(
            flops=4 * slots * width * quarter, bytes_accessed=10 << 20, transcendentals=0
        ),
        name="experts_act",
    )(tokens, gain, w_gate, w_up)


def far_down(act, downs, capacity):
    slots, _ = act.shape
    per_dev = len(downs)
    columns = downs[0].shape[1]

    def body(a_ref, *refs):
        w_refs, out_ref = refs[:-1], refs[-1]
        value = a_ref[...].astype(F32)
        products = [
            jnp.dot(
                of_expert(value, e, per_dev, capacity).astype(BF),
                w_ref[...],
                preferred_element_type=F32,
            )
            for e, w_ref in enumerate(w_refs)
        ]
        out_ref[...] = of_all(products, capacity).astype(BF)

    return pl.pallas_call(
        body,
        out_shape=jax.ShapeDtypeStruct((slots, columns), BF),
        in_specs=whole(1 + per_dev),
        out_specs=pl.BlockSpec(memory_space=pltpu.VMEM),
        compiler_params=pltpu.CompilerParams(vmem_limit_bytes=24 << 20),
        name="far_down",
    )(act, *downs)


def experts_down(acts, downs, far, capacity, roles):
    count = len(acts)
    slots, quarter = acts[0].shape
    per_dev = len(downs[0])
    columns = downs[0][0].shape[1]
    piece = columns // roles

    def body(*refs):
        a_refs, w_refs, (far_ref, out_ref) = refs[:count], refs[count:-2], refs[-2:]
        ones = [
            [of_expert(a[...].astype(F32), e, per_dev, capacity).astype(BF) for e in range(per_dev)]
            for a in a_refs
        ]
        for s in range(roles):
            totals = []
            for e in range(per_dev):
                total = None
                for i in range(count):
                    product = jnp.dot(
                        ones[i][e],
                        w_refs[i * per_dev + e][:, s * piece : (s + 1) * piece],
                        preferred_element_type=F32,
                    )
                    total = product if total is None else total + product
                totals.append(total)
            total = of_all(totals, capacity) + far_ref[:, s * piece : (s + 1) * piece].astype(F32)
            out_ref[s * slots : (s + 1) * slots] = total.astype(BF)

    flat = [w for each in downs for w in each]
    return pl.pallas_call(
        body,
        out_shape=jax.ShapeDtypeStruct((roles * slots, piece), BF),
        in_specs=whole(count + len(flat) + 1),
        out_specs=pl.BlockSpec(memory_space=pltpu.VMEM),
        compiler_params=pltpu.CompilerParams(vmem_limit_bytes=24 << 20),
        cost_estimate=pl.CostEstimate(
            flops=2 * slots * count * quarter * columns, bytes_accessed=5 << 20, transcendentals=0
        ),
        name="experts_down",
    )(*acts, *flat, far)


def per_device(
    queries,
    k_cache,
    value_cache,
    new_token_key,
    new_token_value,
    lengths,
    output_weight,
    residual,
    norm_gain,
    routes,
    route_scores,
    w_gate,
    w_up,
    w_down,
):
    rows_here = queries.shape[0]
    width = residual.shape[1]
    roles = lax.axis_size("role")
    heads_count = lax.axis_size("heads")
    shards = lax.axis_size("rows")
    half = width // roles
    piece = half // heads_count
    per_dev, _, quarter = w_gate.shape
    experts = per_dev * shards * roles
    capacity = 8
    role = lax.axis_index("role")
    head = lax.axis_index("heads")
    swap = [(i, roles - 1 - i) for i in range(roles)]

    def shift(x, step):
        return lax.ppermute(
            x, "heads", [(i, (i + step) % heads_count) for i in range(heads_count)]
        )

    theirs, mine = attend(
        queries[:, 0, 0],
        k_cache[:, 0],
        value_cache[:, 0],
        new_token_key[:, 0],
        new_token_value[:, 0],
        lengths,
        output_weight[0, 0],
        role,
    )
    received = lax.ppermute(theirs, "role", swap)
    chip = (mine + received.astype(F32)).astype(BF)
    chip, w_down = lax.optimization_barrier((chip, w_down))
    across, near = heads_count // 2, (0, 1, heads_count - 1)
    pieces = [(step, e) for step in (*near, across) for e in range(per_dev)]
    rest = cut_down(w_down, head, heads_count, roles, pieces)
    total = chip.astype(F32)
    for step in range(1, heads_count):
        total = total + shift(chip, step).astype(F32)
    first = role == 0
    resid = jnp.where(first, residual[:, :half], residual[:, half:]).astype(F32)
    gain = jnp.where(first, norm_gain[:half], norm_gain[half:])
    hidden = resid + total
    hidden, *rest = lax.optimization_barrier((hidden, *rest))
    downs = [
        [shift(part, step) if step else part for part in rest[i * per_dev : (i + 1) * per_dev]]
        for i, step in enumerate(near)
    ]
    scaled = (hidden * gain).astype(BF)

    named = routes[:, :, None] == jnp.arange(experts, dtype=jnp.int32)
    chosen = jnp.any(named, axis=1)
    shares = route_scores / jnp.sum(route_scores, axis=1, keepdims=True)
    coef = jnp.sum(jnp.where(named, shares[:, :, None], F32(0.0)), axis=1)
    order = jnp.arange(rows_here, dtype=jnp.int32)
    before = (order[None, :] < order[:, None]).astype(BF)
    rank = jnp.dot(before, chosen.astype(BF), preferred_element_type=F32).astype(jnp.int32)
    taken = chosen[:, :, None] & (rank[:, :, None] == jnp.arange(capacity, dtype=jnp.int32))
    slots = experts * capacity
    pick = taken.reshape(rows_here, slots).astype(BF)
    mixing = jnp.where(taken, coef[:, :, None], F32(0.0)).reshape(rows_here, slots)

    outgoing = lax.dot_general(
        pick, scaled, (((0,), (0,)), ((), ())), preferred_element_type=F32
    ).astype(BF)
    outgoing = outgoing.reshape(roles * shards, per_dev * capacity, half)
    incoming = lax.all_to_all(outgoing, ("role", "rows"), 0, 0, tiled=True)
    tokens = incoming.reshape(roles, shards * per_dev * capacity, half)
    act = experts_act(tokens, norm_gain.reshape(roles, 1, half), w_gate, w_up, capacity)
    far = shift(far_down(act, rest[len(near) * per_dev :], capacity), across)
    acts = [shift(act, step) if step else act for step in near]
    result = experts_down(acts, downs, far, capacity, roles)
    result = result.reshape(roles * shards, per_dev * capacity, piece)
    returned = lax.all_to_all(result, ("role", "rows"), 0, 0, tiled=True)
    returned = returned.reshape(slots, piece)
    mix_high = mixing.astype(BF)
    mix_low = (mixing - mix_high.astype(F32)).astype(BF)
    moe = jnp.dot(mix_high, returned, preferred_element_type=F32) + jnp.dot(
        mix_low, returned, preferred_element_type=F32
    )
    own = lax.dynamic_slice_in_dim(hidden, head * piece, piece, 1)
    return (own + moe).astype(BF)


def solution(mesh):
    in_specs = (
        P("rows", "role", "heads", None),
        P("rows", "heads", None, None),
        P("rows", "heads", None, None),
        P("rows", "heads", None),
        P("rows", "heads", None),
        P("rows"),
        P("role", "heads", None, None),
        P("rows", None),
        P(),
        P("rows", None),
        P("rows", None),
        P(("role", "rows"), None, "heads"),
        P(("role", "rows"), None, "heads"),
        P(("role", "rows"), "heads", None),
    )
    out_specs = P("rows", ("role", "heads"))
    return jax.shard_map(
        per_device, mesh=mesh, in_specs=in_specs, out_specs=out_specs, check_vma=False
    )
```

```python
import math

import jax
import jax.numpy as jnp
from jax import lax
from jax.experimental import pallas as pl
from jax.experimental.pallas import tpu as pltpu
from jax.sharding import PartitionSpec as P

BF = jnp.bfloat16
F32 = jnp.float32
EPS = 1e-06
VMEM = 60 << 20


def whole(n):
    return [pl.BlockSpec(memory_space=pltpu.VMEM)] * n


def cut_down(w_down, head, heads_count, roles, pieces):
    per_dev, quarter, width = w_down.shape
    half = width // roles
    piece = half // heads_count
    parts = 4
    count = len(pieces)

    def body(head_ref, w_hbm, *rest):
        outs, w_ref, in_sems, out_sems = rest[:count], *rest[count:]
        loads, stores = [], []
        for e in range(per_dev):
            for i in range(parts):
                rows = pl.ds(i * (quarter // parts), quarter // parts)
                loads.append(
                    pltpu.make_async_copy(
                        w_hbm.at[e, rows], w_ref.at[e, rows], in_sems.at[e * parts + i]
                    )
                )
        for i, (step, e) in enumerate(pieces):
            place = lax.rem(head_ref[0] + step, heads_count)
            for s in range(roles):
                start = pl.multiple_of(s * half + place * piece, piece)
                stores.append(
                    pltpu.make_async_copy(
                        w_ref.at[e, :, pl.ds(start, piece)],
                        outs[i].at[:, pl.ds(s * piece, piece)],
                        out_sems.at[i * roles + s],
                    )
                )
        for load in loads:
            load.start()
        for e in range(per_dev):
            for load in loads[e * parts : (e + 1) * parts]:
                load.wait()
            for i, (_, mine) in enumerate(pieces):
                if mine == e:
                    for store in stores[i * roles : (i + 1) * roles]:
                        store.start()
        for store in stores:
            store.wait()

    return pl.pallas_call(
        body,
        out_shape=[jax.ShapeDtypeStruct((quarter, roles * piece), BF)] * count,
        in_specs=[pl.BlockSpec(memory_space=pltpu.SMEM), pl.BlockSpec(memory_space=pltpu.HBM)],
        out_specs=[pl.BlockSpec(memory_space=pltpu.HBM)] * count,
        scratch_shapes=[
            pltpu.VMEM(w_down.shape, BF),
            pltpu.SemaphoreType.DMA((per_dev * parts,)),
            pltpu.SemaphoreType.DMA((count * roles,)),
        ],
        compiler_params=pltpu.CompilerParams(vmem_limit_bytes=VMEM),
        cost_estimate=pl.CostEstimate(
            flops=0, bytes_accessed=2 * w_down.size * 2, transcendentals=0
        ),
        name="cut_down",
    )(head.reshape(1), w_down)


def attend(queries, k_cache, value_cache, new_key, new_value, lengths, output_weight, role):
    rows, depth = queries.shape
    cache, size = k_cache.shape[1:]
    group = depth // size
    width = output_weight.shape[1]
    half = width // 2
    step = 16
    blocks = rows // step
    scale = 1.0 / math.sqrt(size)

    def body(
        role_ref, len_ref, q_ref, k_hbm, v_hbm, nk_ref, nv_ref, w_hbm,
        theirs_ref, mine_ref, k_ref, v_ref, w_ref, attn_ref, k_sem, v_sem, w_sem,
    ):
        def copy(hbm, ref, sem, i):
            place = pl.ds(i * step, step)
            return pltpu.make_async_copy(hbm.at[place], ref.at[place], sem.at[i])

        weights = []
        for s in range(2):
            side = role_ref[0] if s else 1 - role_ref[0]
            start = pl.multiple_of(side * half, half)
            for i in range(4):
                place = pl.ds(i * (depth // 4), depth // 4)
                weights.append(
                    pltpu.make_async_copy(
                        w_hbm.at[place, pl.ds(start, half)],
                        w_ref.at[s, place],
                        w_sem.at[4 * s + i],
                    )
                )
        for i in range(blocks):
            copy(k_hbm, k_ref, k_sem, i).start()
            copy(v_hbm, v_ref, v_sem, i).start()
        for i in range(blocks):
            place = slice(i * step, (i + 1) * step)
            q = q_ref[place].reshape(step, group, size)
            copy(k_hbm, k_ref, k_sem, i).wait()
            if i == 0:
                for weight in weights:
                    weight.start()
            scores = lax.dot_general(
                q, k_ref[place], (((2,), (2,)), ((0,), (0,))), preferred_element_type=F32
            )
            scores = scores * scale
            fresh = jnp.sum(
                q.astype(F32) * nk_ref[place].astype(F32)[:, None, :], axis=2, keepdims=True
            )
            fresh = fresh * scale
            position = lax.broadcasted_iota(jnp.int32, (step, group, cache), 2)
            row = lax.broadcasted_iota(jnp.int32, (step, group, cache), 0)
            limit = jnp.full((step, group, cache), len_ref[i * step])
            for j in range(1, step):
                limit = jnp.where(row == j, len_ref[i * step + j], limit)
            scores = jnp.where(position < limit, scores, -jnp.inf)
            top = jnp.maximum(jnp.max(scores, axis=2, keepdims=True), fresh)
            expo = jnp.exp(scores - top)
            expo_new = jnp.exp(fresh - top)
            inverse = 1.0 / (jnp.sum(expo, axis=2, keepdims=True) + expo_new)
            probs = (expo * inverse).astype(BF)
            probs_new = (expo_new * inverse).astype(BF).astype(F32)
            copy(v_hbm, v_ref, v_sem, i).wait()
            result = lax.dot_general(
                probs, v_ref[place], (((2,), (1,)), ((0,), (0,))), preferred_element_type=F32
            )
            result = result + probs_new * nv_ref[place].astype(F32)[:, None, :]
            attn_ref[place, :] = result.reshape(step, depth).astype(BF)
        for weight in weights[:4]:
            weight.wait()
        product = jnp.dot(attn_ref[...], w_ref[0], preferred_element_type=F32)
        theirs_ref[...] = product.astype(BF)
        for weight in weights[4:]:
            weight.wait()
        mine_ref[...] = jnp.dot(attn_ref[...], w_ref[1], preferred_element_type=F32)

    return pl.pallas_call(
        body,
        out_shape=[
            jax.ShapeDtypeStruct((rows, half), BF),
            jax.ShapeDtypeStruct((rows, half), F32),
        ],
        in_specs=[
            pl.BlockSpec(memory_space=pltpu.SMEM),
            pl.BlockSpec(memory_space=pltpu.SMEM),
            pl.BlockSpec(memory_space=pltpu.VMEM),
            pl.BlockSpec(memory_space=pltpu.HBM),
            pl.BlockSpec(memory_space=pltpu.HBM),
            pl.BlockSpec(memory_space=pltpu.VMEM),
            pl.BlockSpec(memory_space=pltpu.VMEM),
            pl.BlockSpec(memory_space=pltpu.HBM),
        ],
        out_specs=whole(2),
        scratch_shapes=[
            pltpu.VMEM((rows, cache, size), BF),
            pltpu.VMEM((rows, cache, size), BF),
            pltpu.VMEM((2, depth, half), BF),
            pltpu.VMEM((rows, depth), BF),
            pltpu.SemaphoreType.DMA((blocks,)),
            pltpu.SemaphoreType.DMA((blocks,)),
            pltpu.SemaphoreType.DMA((8,)),
        ],
        compiler_params=pltpu.CompilerParams(vmem_limit_bytes=57 << 20),
        cost_estimate=pl.CostEstimate(
            flops=0, bytes_accessed=1 << 20, transcendentals=0
        ),
        name="attend",
    )(role.reshape(1), lengths, queries, k_cache, value_cache, new_key, new_value, output_weight)


def of_expert(value, e, per_dev, capacity):
    rows, columns = value.shape
    blocks = rows // (per_dev * capacity)
    return value.reshape(blocks, per_dev, capacity, columns)[:, e].reshape(
        blocks * capacity, columns
    )


def of_all(values, capacity):
    rows, columns = values[0].shape
    blocks = rows // capacity
    parts = [v.reshape(blocks, 1, capacity, columns) for v in values]
    return jnp.concatenate(parts, axis=1).reshape(len(values) * rows, columns)


def experts_act(tokens, gain, w_gate, w_up, capacity):
    roles, slots, half = tokens.shape
    per_dev, width, quarter = w_gate.shape
    chunk = 512

    def body(x_ref, gain_ref, g_any, u_any, act_ref, g_ref, u_ref, sums, sems):
        copies = []
        for k in range(width // chunk):
            rows = pl.ds(k * chunk, chunk)
            copies.append(
                [
                    pltpu.make_async_copy(
                        source.at[:, rows], target.at[:, rows], sems.at[2 * k + i]
                    )
                    for i, (source, target) in enumerate(((g_any, g_ref), (u_any, u_ref)))
                ]
            )
        for pair in copies:
            for copy in pair:
                copy.start()
        square = jnp.zeros((slots, 1), F32)
        for k in range(width // chunk):
            s, place = divmod(k * chunk, half)
            x = x_ref[s, :, place : place + chunk].astype(F32)
            plain = x * (1.0 / gain_ref[s, :, place : place + chunk])
            square = square + jnp.sum(plain * plain, axis=1, keepdims=True)
            for copy in copies[k]:
                copy.wait()
            for e in range(per_dev):
                one = of_expert(x, e, per_dev, capacity).astype(BF)
                for i, w_ref in enumerate((g_ref, u_ref)):
                    product = jnp.dot(
                        one, w_ref[e, k * chunk : (k + 1) * chunk], preferred_element_type=F32
                    )
                    if k:
                        product = product + sums[2 * e + i]
                    sums[2 * e + i] = product
        inverse = lax.rsqrt(square / width + EPS)
        gate = of_all([sums[2 * e] for e in range(per_dev)], capacity) * inverse
        upper = of_all([sums[2 * e + 1] for e in range(per_dev)], capacity) * inverse
        act_ref[...] = (gate / (1.0 + jnp.exp(-gate)) * upper).astype(BF)

    return pl.pallas_call(
        body,
        out_shape=jax.ShapeDtypeStruct((slots, quarter), BF),
        in_specs=whole(2) + [pl.BlockSpec(memory_space=pltpu.HBM)] * 2,
        out_specs=pl.BlockSpec(memory_space=pltpu.VMEM),
        scratch_shapes=[
            pltpu.VMEM(w_gate.shape, BF),
            pltpu.VMEM(w_up.shape, BF),
            pltpu.VMEM((2 * per_dev, slots // per_dev, quarter), F32),
            pltpu.SemaphoreType.DMA((2 * (width // chunk),)),
        ],
        compiler_params=pltpu.CompilerParams(vmem_limit_bytes=49 << 20),
        cost_estimate=pl.CostEstimate(
            flops=4 * slots * width * quarter, bytes_accessed=10 << 20, transcendentals=0
        ),
        name="experts_act",
    )(tokens, gain, w_gate, w_up)


def far_down(act, downs, capacity):
    slots, _ = act.shape
    per_dev = len(downs)
    columns = downs[0].shape[1]

    def body(a_ref, *refs):
        w_refs, out_ref = refs[:-1], refs[-1]
        value = a_ref[...].astype(F32)
        products = [
            jnp.dot(
                of_expert(value, e, per_dev, capacity).astype(BF),
                w_ref[...],
                preferred_element_type=F32,
            )
            for e, w_ref in enumerate(w_refs)
        ]
        out_ref[...] = of_all(products, capacity).astype(BF)

    return pl.pallas_call(
        body,
        out_shape=jax.ShapeDtypeStruct((slots, columns), BF),
        in_specs=whole(1 + per_dev),
        out_specs=pl.BlockSpec(memory_space=pltpu.VMEM),
        compiler_params=pltpu.CompilerParams(vmem_limit_bytes=24 << 20),
        name="far_down",
    )(act, *downs)


def own_down(act, own, others, capacity):
    slots, _ = act.shape
    per_dev = len(own)
    rows = slots // per_dev
    columns = own[0].shape[1]
    count = len(others)

    def body(a_ref, *refs):
        w_refs, sources = refs[:per_dev], refs[per_dev : per_dev + count]
        out_ref, targets, sems = refs[per_dev + count], refs[per_dev + count + 1 : -1], refs[-1]
        copies = [
            pltpu.make_async_copy(source, target, sems.at[i])
            for i, (source, target) in enumerate(zip(sources, targets))
        ]
        for copy in copies:
            copy.start()
        value = a_ref[...].astype(F32)
        for e in range(per_dev):
            out_ref[e * rows : (e + 1) * rows] = jnp.dot(
                of_expert(value, e, per_dev, capacity).astype(BF),
                w_refs[e][...],
                preferred_element_type=F32,
            )
        for copy in copies:
            copy.wait()

    return pl.pallas_call(
        body,
        out_shape=[jax.ShapeDtypeStruct((slots, columns), F32)]
        + [jax.ShapeDtypeStruct(w.shape, BF) for w in others],
        in_specs=whole(1 + per_dev) + [pl.BlockSpec(memory_space=pltpu.HBM)] * count,
        out_specs=whole(1 + count),
        scratch_shapes=[pltpu.SemaphoreType.DMA((count,))],
        compiler_params=pltpu.CompilerParams(vmem_limit_bytes=44 << 20),
        name="own_down",
    )(act, *own, *others)


def experts_down(acts, downs, own, far, capacity, roles):
    count = len(acts)
    slots, _ = acts[0].shape
    per_dev = len(downs[0])
    rows = slots // per_dev
    columns = far.shape[1]
    piece = columns // roles

    def body(*refs):
        a_refs, w_refs = refs[:count], refs[count:-3]
        own_ref, far_ref, out_ref = refs[-3:]
        ones = [
            [of_expert(a[...].astype(F32), e, per_dev, capacity).astype(BF) for e in range(per_dev)]
            for a in a_refs
        ]
        for s in range(roles):
            place = slice(s * piece, (s + 1) * piece)
            totals = []
            for e in range(per_dev):
                total = own_ref[e * rows : (e + 1) * rows, place]
                for i in range(count):
                    total = total + jnp.dot(
                        ones[i][e],
                        w_refs[i * per_dev + e][:, place],
                        preferred_element_type=F32,
                    )
                totals.append(total)
            total = of_all(totals, capacity) + far_ref[:, place].astype(F32)
            out_ref[s * slots : (s + 1) * slots] = total.astype(BF)

    flat = [w for each in downs for w in each]
    return pl.pallas_call(
        body,
        out_shape=jax.ShapeDtypeStruct((roles * slots, piece), BF),
        in_specs=whole(count + len(flat) + 2),
        out_specs=pl.BlockSpec(memory_space=pltpu.VMEM),
        compiler_params=pltpu.CompilerParams(vmem_limit_bytes=24 << 20),
        name="experts_down",
    )(*acts, *flat, own, far)


def per_device(
    queries,
    k_cache,
    value_cache,
    new_token_key,
    new_token_value,
    lengths,
    output_weight,
    residual,
    norm_gain,
    routes,
    route_scores,
    w_gate,
    w_up,
    w_down,
):
    rows_here = queries.shape[0]
    width = residual.shape[1]
    roles = lax.axis_size("role")
    heads_count = lax.axis_size("heads")
    shards = lax.axis_size("rows")
    half = width // roles
    piece = half // heads_count
    per_dev, _, quarter = w_gate.shape
    experts = per_dev * shards * roles
    capacity = 8
    role = lax.axis_index("role")
    head = lax.axis_index("heads")
    swap = [(i, roles - 1 - i) for i in range(roles)]

    def shift(x, step):
        return lax.ppermute(
            x, "heads", [(i, (i + step) % heads_count) for i in range(heads_count)]
        )

    theirs, mine = attend(
        queries[:, 0, 0],
        k_cache[:, 0],
        value_cache[:, 0],
        new_token_key[:, 0],
        new_token_value[:, 0],
        lengths,
        output_weight[0, 0],
        role,
    )
    received = lax.ppermute(theirs, "role", swap)
    chip = (mine + received.astype(F32)).astype(BF)
    chip, w_down = lax.optimization_barrier((chip, w_down))
    across, near = heads_count // 2, (0, 1, heads_count - 1)
    pieces = [(step, e) for step in (*near, across) for e in range(per_dev)]
    rest = cut_down(w_down, head, heads_count, roles, pieces)
    total = chip.astype(F32)
    for step in range(1, heads_count):
        total = total + shift(chip, step).astype(F32)
    first = role == 0
    resid = jnp.where(first, residual[:, :half], residual[:, half:]).astype(F32)
    gain = jnp.where(first, norm_gain[:half], norm_gain[half:])
    hidden = resid + total
    hidden, *rest = lax.optimization_barrier((hidden, *rest))
    downs = [
        [shift(part, step) if step else part for part in rest[i * per_dev : (i + 1) * per_dev]]
        for i, step in enumerate(near)
    ]
    scaled = (hidden * gain).astype(BF)

    named = routes[:, :, None] == jnp.arange(experts, dtype=jnp.int32)
    chosen = jnp.any(named, axis=1)
    shares = route_scores / jnp.sum(route_scores, axis=1, keepdims=True)
    coef = jnp.sum(jnp.where(named, shares[:, :, None], F32(0.0)), axis=1)
    order = jnp.arange(rows_here, dtype=jnp.int32)
    before = (order[None, :] < order[:, None]).astype(BF)
    rank = jnp.dot(before, chosen.astype(BF), preferred_element_type=F32).astype(jnp.int32)
    taken = chosen[:, :, None] & (rank[:, :, None] == jnp.arange(capacity, dtype=jnp.int32))
    slots = experts * capacity
    pick = taken.reshape(rows_here, slots).astype(BF)
    mixing = jnp.where(taken, coef[:, :, None], F32(0.0)).reshape(rows_here, slots)

    outgoing = lax.dot_general(
        pick, scaled, (((0,), (0,)), ((), ())), preferred_element_type=F32
    ).astype(BF)
    outgoing = outgoing.reshape(roles * shards, per_dev * capacity, half)
    incoming = lax.all_to_all(outgoing, ("role", "rows"), 0, 0, tiled=True)
    tokens = incoming.reshape(roles, shards * per_dev * capacity, half)
    act = experts_act(tokens, norm_gain.reshape(roles, 1, half), w_gate, w_up, capacity)
    far = shift(far_down(act, rest[len(near) * per_dev :], capacity), across)
    acts = [shift(act, step) for step in near[1:]]
    others = [w for each in downs[1:] for w in each]
    act, *others = lax.optimization_barrier((act, *others))
    own, *others = own_down(act, downs[0], others, capacity)
    others = [others[i : i + per_dev] for i in range(0, len(others), per_dev)]
    result = experts_down(acts, others, own, far, capacity, roles)
    result = result.reshape(roles * shards, per_dev * capacity, piece)
    returned = lax.all_to_all(result, ("role", "rows"), 0, 0, tiled=True)
    returned = returned.reshape(slots, piece)
    mix_high = mixing.astype(BF)
    mix_low = (mixing - mix_high.astype(F32)).astype(BF)
    moe = jnp.dot(mix_high, returned, preferred_element_type=F32) + jnp.dot(
        mix_low, returned, preferred_element_type=F32
    )
    own = lax.dynamic_slice_in_dim(hidden, head * piece, piece, 1)
    return (own + moe).astype(BF)


def solution(mesh):
    in_specs = (
        P("rows", "role", "heads", None),
        P("rows", "heads", None, None),
        P("rows", "heads", None, None),
        P("rows", "heads", None),
        P("rows", "heads", None),
        P("rows"),
        P("role", "heads", None, None),
        P("rows", None),
        P(),
        P("rows", None),
        P("rows", None),
        P(("role", "rows"), None, "heads"),
        P(("role", "rows"), None, "heads"),
        P(("role", "rows"), "heads", None),
    )
    out_specs = P("rows", ("role", "heads"))
    return jax.shard_map(
        per_device, mesh=mesh, in_specs=in_specs, out_specs=out_specs, check_vma=False
    )
```

```python
import math

import jax
import jax.numpy as jnp
from jax import lax
from jax.experimental import pallas as pl
from jax.experimental.pallas import tpu as pltpu
from jax.sharding import PartitionSpec as P

BF = jnp.bfloat16
F32 = jnp.float32
EPS = 1e-06
VMEM = 60 << 20


def whole(n):
    return [pl.BlockSpec(memory_space=pltpu.VMEM)] * n


def cut_down(w_down, head, heads_count, roles, pieces):
    per_dev, quarter, width = w_down.shape
    half = width // roles
    piece = half // heads_count
    parts = 4
    count = len(pieces)

    def body(head_ref, w_hbm, *rest):
        outs, w_ref, in_sems, out_sems = rest[:count], *rest[count:]
        loads, stores = [], []
        for e in range(per_dev):
            for i in range(parts):
                rows = pl.ds(i * (quarter // parts), quarter // parts)
                loads.append(
                    pltpu.make_async_copy(
                        w_hbm.at[e, rows], w_ref.at[e, rows], in_sems.at[e * parts + i]
                    )
                )
        for i, (step, e) in enumerate(pieces):
            place = lax.rem(head_ref[0] + step, heads_count)
            for s in range(roles):
                start = pl.multiple_of(s * half + place * piece, piece)
                stores.append(
                    pltpu.make_async_copy(
                        w_ref.at[e, :, pl.ds(start, piece)],
                        outs[i].at[:, pl.ds(s * piece, piece)],
                        out_sems.at[i * roles + s],
                    )
                )
        for load in loads:
            load.start()
        for e in range(per_dev):
            for load in loads[e * parts : (e + 1) * parts]:
                load.wait()
            for i, (_, mine) in enumerate(pieces):
                if mine == e:
                    for store in stores[i * roles : (i + 1) * roles]:
                        store.start()
        for store in stores:
            store.wait()

    return pl.pallas_call(
        body,
        out_shape=[jax.ShapeDtypeStruct((quarter, roles * piece), BF)] * count,
        in_specs=[pl.BlockSpec(memory_space=pltpu.SMEM), pl.BlockSpec(memory_space=pltpu.HBM)],
        out_specs=[pl.BlockSpec(memory_space=pltpu.HBM)] * count,
        scratch_shapes=[
            pltpu.VMEM(w_down.shape, BF),
            pltpu.SemaphoreType.DMA((per_dev * parts,)),
            pltpu.SemaphoreType.DMA((count * roles,)),
        ],
        compiler_params=pltpu.CompilerParams(vmem_limit_bytes=VMEM),
        cost_estimate=pl.CostEstimate(
            flops=0, bytes_accessed=2 * w_down.size * 2, transcendentals=0
        ),
        name="cut_down",
    )(head.reshape(1), w_down)


def attend(queries, k_cache, value_cache, new_key, new_value, lengths, output_weight, role):
    rows, depth = queries.shape
    cache, size = k_cache.shape[1:]
    group = depth // size
    width = output_weight.shape[1]
    half = width // 2
    step = 16
    blocks = rows // step
    scale = 1.0 / math.sqrt(size)

    def body(
        role_ref, len_ref, q_ref, k_hbm, v_hbm, nk_ref, nv_ref, w_hbm,
        theirs_ref, mine_ref, k_ref, v_ref, w_ref, attn_ref, k_sem, v_sem, w_sem,
    ):
        def copy(hbm, ref, sem, i):
            place = pl.ds(i * step, step)
            return pltpu.make_async_copy(hbm.at[place], ref.at[place], sem.at[i])

        weights = []
        for s in range(2):
            side = role_ref[0] if s else 1 - role_ref[0]
            start = pl.multiple_of(side * half, half)
            for i in range(4):
                place = pl.ds(i * (depth // 4), depth // 4)
                weights.append(
                    pltpu.make_async_copy(
                        w_hbm.at[place, pl.ds(start, half)],
                        w_ref.at[s, place],
                        w_sem.at[4 * s + i],
                    )
                )
        for i in range(blocks):
            copy(k_hbm, k_ref, k_sem, i).start()
            copy(v_hbm, v_ref, v_sem, i).start()
        for i in range(blocks):
            place = slice(i * step, (i + 1) * step)
            q = q_ref[place].reshape(step, group, size)
            copy(k_hbm, k_ref, k_sem, i).wait()
            if i == 0:
                for weight in weights:
                    weight.start()
            scores = lax.dot_general(
                q, k_ref[place], (((2,), (2,)), ((0,), (0,))), preferred_element_type=F32
            )
            scores = scores * scale
            fresh = jnp.sum(
                q.astype(F32) * nk_ref[place].astype(F32)[:, None, :], axis=2, keepdims=True
            )
            fresh = fresh * scale
            position = lax.broadcasted_iota(jnp.int32, (step, group, cache), 2)
            row = lax.broadcasted_iota(jnp.int32, (step, group, cache), 0)
            limit = jnp.full((step, group, cache), len_ref[i * step])
            for j in range(1, step):
                limit = jnp.where(row == j, len_ref[i * step + j], limit)
            scores = jnp.where(position < limit, scores, -jnp.inf)
            top = jnp.maximum(jnp.max(scores, axis=2, keepdims=True), fresh)
            expo = jnp.exp(scores - top)
            expo_new = jnp.exp(fresh - top)
            inverse = 1.0 / (jnp.sum(expo, axis=2, keepdims=True) + expo_new)
            probs = (expo * inverse).astype(BF)
            probs_new = (expo_new * inverse).astype(BF).astype(F32)
            copy(v_hbm, v_ref, v_sem, i).wait()
            result = lax.dot_general(
                probs, v_ref[place], (((2,), (1,)), ((0,), (0,))), preferred_element_type=F32
            )
            result = result + probs_new * nv_ref[place].astype(F32)[:, None, :]
            attn_ref[place, :] = result.reshape(step, depth).astype(BF)
        for weight in weights[:4]:
            weight.wait()
        product = jnp.dot(attn_ref[...], w_ref[0], preferred_element_type=F32)
        theirs_ref[...] = product.astype(BF)
        for weight in weights[4:]:
            weight.wait()
        mine_ref[...] = jnp.dot(attn_ref[...], w_ref[1], preferred_element_type=F32)

    return pl.pallas_call(
        body,
        out_shape=[
            jax.ShapeDtypeStruct((rows, half), BF),
            jax.ShapeDtypeStruct((rows, half), F32),
        ],
        in_specs=[
            pl.BlockSpec(memory_space=pltpu.SMEM),
            pl.BlockSpec(memory_space=pltpu.SMEM),
            pl.BlockSpec(memory_space=pltpu.VMEM),
            pl.BlockSpec(memory_space=pltpu.HBM),
            pl.BlockSpec(memory_space=pltpu.HBM),
            pl.BlockSpec(memory_space=pltpu.VMEM),
            pl.BlockSpec(memory_space=pltpu.VMEM),
            pl.BlockSpec(memory_space=pltpu.HBM),
        ],
        out_specs=whole(2),
        scratch_shapes=[
            pltpu.VMEM((rows, cache, size), BF),
            pltpu.VMEM((rows, cache, size), BF),
            pltpu.VMEM((2, depth, half), BF),
            pltpu.VMEM((rows, depth), BF),
            pltpu.SemaphoreType.DMA((blocks,)),
            pltpu.SemaphoreType.DMA((blocks,)),
            pltpu.SemaphoreType.DMA((8,)),
        ],
        compiler_params=pltpu.CompilerParams(vmem_limit_bytes=57 << 20),
        cost_estimate=pl.CostEstimate(
            flops=0, bytes_accessed=1 << 20, transcendentals=0
        ),
        name="attend",
    )(role.reshape(1), lengths, queries, k_cache, value_cache, new_key, new_value, output_weight)


def of_expert(value, e, per_dev, capacity):
    rows, columns = value.shape
    blocks = rows // (per_dev * capacity)
    return value.reshape(blocks, per_dev, capacity, columns)[:, e].reshape(
        blocks * capacity, columns
    )


def of_all(values, capacity):
    rows, columns = values[0].shape
    blocks = rows // capacity
    parts = [v.reshape(blocks, 1, capacity, columns) for v in values]
    return jnp.concatenate(parts, axis=1).reshape(len(values) * rows, columns)


def expert_act(tokens, gain, w_gate, w_up, across, e, before, capacity):
    roles, slots, half = tokens.shape
    per_dev, width, quarter = w_gate.shape
    columns = across.shape[1]
    chunk = 512
    rows = slots // per_dev
    done = e * rows

    def body(x_ref, gain_ref, g_hbm, u_hbm, w_ref, *rest):
        before_ref = rest[0] if e else None
        act_ref, far_ref, g_ref, u_ref, sums, sems = rest[1 if e else 0 :]
        copies = []
        for k in range(width // chunk):
            place = pl.ds(k * chunk, chunk)
            copies.append(
                [
                    pltpu.make_async_copy(hbm.at[e, place], ref.at[place], sems.at[2 * k + i])
                    for i, (hbm, ref) in enumerate(((g_hbm, g_ref), (u_hbm, u_ref)))
                ]
            )
        for pair in copies:
            for copy in pair:
                copy.start()
        square = jnp.zeros((rows, 1), F32)
        for k in range(width // chunk):
            s, place = divmod(k * chunk, half)
            x = x_ref[s, :, place : place + chunk].astype(F32)
            x = of_expert(x, e, per_dev, capacity)
            plain = x * (1.0 / gain_ref[s, :, place : place + chunk])
            square = square + jnp.sum(plain * plain, axis=1, keepdims=True)
            x = x.astype(BF)
            for copy in copies[k]:
                copy.wait()
            for i, ref in enumerate((g_ref, u_ref)):
                product = jnp.dot(
                    x, ref[k * chunk : (k + 1) * chunk], preferred_element_type=F32
                )
                sums[i] = product + sums[i] if k else product
        inverse = lax.rsqrt(square / width + EPS)
        gate, upper = sums[0] * inverse, sums[1] * inverse
        act = (gate / (1.0 + jnp.exp(-gate)) * upper).astype(BF)
        if e:
            act_ref[:done] = before_ref[...]
        act_ref[done:] = act
        far_ref[...] = jnp.dot(act, w_ref[...], preferred_element_type=F32).astype(BF)

    return pl.pallas_call(
        body,
        out_shape=[
            jax.ShapeDtypeStruct((done + rows, quarter), BF),
            jax.ShapeDtypeStruct((rows, columns), BF),
        ],
        in_specs=whole(2)
        + [pl.BlockSpec(memory_space=pltpu.HBM)] * 2
        + whole(2 if e else 1),
        out_specs=whole(2),
        scratch_shapes=[
            pltpu.VMEM((width, quarter), BF),
            pltpu.VMEM((width, quarter), BF),
            pltpu.VMEM((2, rows, quarter), F32),
            pltpu.SemaphoreType.DMA((2 * (width // chunk),)),
        ],
        compiler_params=pltpu.CompilerParams(vmem_limit_bytes=49 << 20),
        cost_estimate=pl.CostEstimate(
            flops=4 * rows * width * quarter, bytes_accessed=6 << 20, transcendentals=0
        ),
        name=f"expert_act_{e}",
    )(tokens, gain, w_gate, w_up, across, *([before] if e else []))


def own_down(act, own, others, fars):
    slots, _ = act.shape
    per_dev = len(own)
    rows = slots // per_dev
    columns = own[0].shape[1]
    count, early = len(others), len(fars)

    def body(a_ref, *refs):
        w_refs, sources = refs[:per_dev], refs[per_dev : per_dev + count]
        far_refs, (out_ref, *targets, sems) = refs[per_dev + count :][:early], refs[per_dev + count + early :]
        copies = [
            pltpu.make_async_copy(source, target, sems.at[i])
            for i, (source, target) in enumerate(zip(sources, targets))
        ]
        for copy in copies:
            copy.start()
        for e in range(per_dev):
            place = slice(e * rows, (e + 1) * rows)
            value = jnp.dot(a_ref[place], w_refs[e][...], preferred_element_type=F32)
            if e < early:
                value = value + far_refs[e][...].astype(F32)
            out_ref[place] = value
        for copy in copies:
            copy.wait()

    return pl.pallas_call(
        body,
        out_shape=[jax.ShapeDtypeStruct((slots, columns), F32)]
        + [jax.ShapeDtypeStruct(w.shape, BF) for w in others],
        in_specs=whole(1 + per_dev)
        + [pl.BlockSpec(memory_space=pltpu.HBM)] * count
        + whole(early),
        out_specs=whole(1 + count),
        scratch_shapes=[pltpu.SemaphoreType.DMA((count,))],
        compiler_params=pltpu.CompilerParams(vmem_limit_bytes=44 << 20),
        cost_estimate=pl.CostEstimate(flops=0, bytes_accessed=8 << 20, transcendentals=0),
        name="own_down",
    )(act, *own, *others, *fars)


def experts_down(acts, downs, own, far, capacity, roles):
    count = len(acts)
    slots, _ = acts[0].shape
    per_dev = len(downs[0])
    rows = slots // per_dev
    columns = far.shape[1]
    piece = columns // roles

    def body(*refs):
        a_refs, w_refs = refs[:count], refs[count:-3]
        own_ref, far_ref, out_ref = refs[-3:]
        for s in range(roles):
            place = slice(s * piece, (s + 1) * piece)
            totals = []
            for e in range(per_dev):
                total = own_ref[e * rows : (e + 1) * rows, place]
                for i in range(count):
                    total = total + jnp.dot(
                        a_refs[i][e * rows : (e + 1) * rows],
                        w_refs[i * per_dev + e][:, place],
                        preferred_element_type=F32,
                    )
                if e == per_dev - 1:
                    total = total + far_ref[:, place].astype(F32)
                totals.append(total)
            out_ref[s * slots : (s + 1) * slots] = of_all(totals, capacity).astype(BF)

    flat = [w for each in downs for w in each]
    return pl.pallas_call(
        body,
        out_shape=jax.ShapeDtypeStruct((roles * slots, piece), BF),
        in_specs=whole(count + len(flat) + 2),
        out_specs=pl.BlockSpec(memory_space=pltpu.VMEM),
        compiler_params=pltpu.CompilerParams(vmem_limit_bytes=24 << 20),
        name="experts_down",
    )(*acts, *flat, own, far)


def per_device(
    queries,
    k_cache,
    value_cache,
    new_token_key,
    new_token_value,
    lengths,
    output_weight,
    residual,
    norm_gain,
    routes,
    route_scores,
    w_gate,
    w_up,
    w_down,
):
    rows_here = queries.shape[0]
    width = residual.shape[1]
    roles = lax.axis_size("role")
    heads_count = lax.axis_size("heads")
    shards = lax.axis_size("rows")
    half = width // roles
    piece = half // heads_count
    per_dev, _, quarter = w_gate.shape
    experts = per_dev * shards * roles
    capacity = 8
    role = lax.axis_index("role")
    head = lax.axis_index("heads")
    swap = [(i, roles - 1 - i) for i in range(roles)]

    def shift(x, step):
        return lax.ppermute(
            x, "heads", [(i, (i + step) % heads_count) for i in range(heads_count)]
        )

    theirs, mine = attend(
        queries[:, 0, 0],
        k_cache[:, 0],
        value_cache[:, 0],
        new_token_key[:, 0],
        new_token_value[:, 0],
        lengths,
        output_weight[0, 0],
        role,
    )
    received = lax.ppermute(theirs, "role", swap)
    chip = (mine + received.astype(F32)).astype(BF)
    chip, w_down = lax.optimization_barrier((chip, w_down))
    across, near = heads_count // 2, (0, 1, heads_count - 1)
    pieces = [(step, e) for step in (*near, across) for e in range(per_dev)]
    rest = cut_down(w_down, head, heads_count, roles, pieces)
    total = chip.astype(F32)
    for step in range(1, heads_count):
        total = total + shift(chip, step).astype(F32)
    first = role == 0
    resid = jnp.where(first, residual[:, :half], residual[:, half:]).astype(F32)
    gain = jnp.where(first, norm_gain[:half], norm_gain[half:])
    hidden = resid + total
    hidden, *rest = lax.optimization_barrier((hidden, *rest))
    downs = [
        [shift(part, step) if step else part for part in rest[i * per_dev : (i + 1) * per_dev]]
        for i, step in enumerate(near)
    ]
    scaled = (hidden * gain).astype(BF)

    named = routes[:, :, None] == jnp.arange(experts, dtype=jnp.int32)
    chosen = jnp.any(named, axis=1)
    shares = route_scores / jnp.sum(route_scores, axis=1, keepdims=True)
    coef = jnp.sum(jnp.where(named, shares[:, :, None], F32(0.0)), axis=1)
    order = jnp.arange(rows_here, dtype=jnp.int32)
    before = (order[None, :] < order[:, None]).astype(BF)
    rank = jnp.dot(before, chosen.astype(BF), preferred_element_type=F32).astype(jnp.int32)
    taken = chosen[:, :, None] & (rank[:, :, None] == jnp.arange(capacity, dtype=jnp.int32))
    slots = experts * capacity
    pick = taken.reshape(rows_here, slots).astype(BF)
    mixing = jnp.where(taken, coef[:, :, None], F32(0.0)).reshape(rows_here, slots)

    outgoing = lax.dot_general(
        pick, scaled, (((0,), (0,)), ((), ())), preferred_element_type=F32
    ).astype(BF)
    outgoing = outgoing.reshape(roles * shards, per_dev * capacity, half)
    incoming = lax.all_to_all(outgoing, ("role", "rows"), 0, 0, tiled=True)
    tokens = incoming.reshape(roles, shards * per_dev * capacity, half)
    flat_gain = norm_gain.reshape(roles, 1, half)
    act, fars = None, []
    for e in range(per_dev):
        opposite = rest[len(near) * per_dev + e]
        act, far = expert_act(tokens, flat_gain, w_gate, w_up, opposite, e, act, capacity)
        fars.append(shift(far, across))
    acts = [shift(act, step) for step in near[1:]]
    others = [w for each in downs[1:] for w in each]
    act, *others = lax.optimization_barrier((act, *others))
    own, *others = own_down(act, downs[0], others, fars[:-1])
    others = [others[i : i + per_dev] for i in range(0, len(others), per_dev)]
    result = experts_down(acts, others, own, fars[-1], capacity, roles)
    result = result.reshape(roles * shards, per_dev * capacity, piece)
    returned = lax.all_to_all(result, ("role", "rows"), 0, 0, tiled=True)
    returned = returned.reshape(slots, piece)
    mix_high = mixing.astype(BF)
    mix_low = (mixing - mix_high.astype(F32)).astype(BF)
    moe = jnp.dot(mix_high, returned, preferred_element_type=F32) + jnp.dot(
        mix_low, returned, preferred_element_type=F32
    )
    own = lax.dynamic_slice_in_dim(hidden, head * piece, piece, 1)
    return (own + moe).astype(BF)


def solution(mesh):
    in_specs = (
        P("rows", "role", "heads", None),
        P("rows", "heads", None, None),
        P("rows", "heads", None, None),
        P("rows", "heads", None),
        P("rows", "heads", None),
        P("rows"),
        P("role", "heads", None, None),
        P("rows", None),
        P(),
        P("rows", None),
        P("rows", None),
        P(("role", "rows"), None, "heads"),
        P(("role", "rows"), None, "heads"),
        P(("role", "rows"), "heads", None),
    )
    out_specs = P("rows", ("role", "heads"))
    return jax.shard_map(
        per_device, mesh=mesh, in_specs=in_specs, out_specs=out_specs, check_vma=False
    )
```

```python
import math

import jax
import jax.numpy as jnp
from jax import lax
from jax.experimental import pallas as pl
from jax.experimental.pallas import tpu as pltpu
from jax.sharding import PartitionSpec as P

BF = jnp.bfloat16
F32 = jnp.float32
EPS = 1e-06
VMEM = 60 << 20


def whole(n):
    return [pl.BlockSpec(memory_space=pltpu.VMEM)] * n


def cut_down(w_down, head, heads_count, roles, pieces):
    per_dev, quarter, width = w_down.shape
    half = width // roles
    piece = half // heads_count
    parts = 4
    count = len(pieces)

    def body(head_ref, w_hbm, *rest):
        outs, w_ref, in_sems, out_sems = rest[:count], *rest[count:]
        loads, stores = [], []
        for e in range(per_dev):
            for i in range(parts):
                rows = pl.ds(i * (quarter // parts), quarter // parts)
                loads.append(
                    pltpu.make_async_copy(
                        w_hbm.at[e, rows], w_ref.at[e, rows], in_sems.at[e * parts + i]
                    )
                )
        for i, (step, e) in enumerate(pieces):
            place = lax.rem(head_ref[0] + step, heads_count)
            for s in range(roles):
                start = pl.multiple_of(s * half + place * piece, piece)
                stores.append(
                    pltpu.make_async_copy(
                        w_ref.at[e, :, pl.ds(start, piece)],
                        outs[i].at[:, pl.ds(s * piece, piece)],
                        out_sems.at[i * roles + s],
                    )
                )
        for load in loads:
            load.start()
        for e in range(per_dev):
            for load in loads[e * parts : (e + 1) * parts]:
                load.wait()
            for i, (_, mine) in enumerate(pieces):
                if mine == e:
                    for store in stores[i * roles : (i + 1) * roles]:
                        store.start()
        for store in stores:
            store.wait()

    return pl.pallas_call(
        body,
        out_shape=[jax.ShapeDtypeStruct((quarter, roles * piece), BF)] * count,
        in_specs=[pl.BlockSpec(memory_space=pltpu.SMEM), pl.BlockSpec(memory_space=pltpu.HBM)],
        out_specs=[pl.BlockSpec(memory_space=pltpu.HBM)] * count,
        scratch_shapes=[
            pltpu.VMEM(w_down.shape, BF),
            pltpu.SemaphoreType.DMA((per_dev * parts,)),
            pltpu.SemaphoreType.DMA((count * roles,)),
        ],
        compiler_params=pltpu.CompilerParams(vmem_limit_bytes=VMEM),
        cost_estimate=pl.CostEstimate(
            flops=0, bytes_accessed=2 * w_down.size * 2, transcendentals=0
        ),
        name="cut_down",
    )(head.reshape(1), w_down)


def attend(queries, k_cache, value_cache, new_key, new_value, lengths, output_weight, role):
    rows, depth = queries.shape
    cache, size = k_cache.shape[1:]
    group = depth // size
    width = output_weight.shape[1]
    half = width // 2
    step = 16
    blocks = rows // step
    scale = 1.0 / math.sqrt(size)

    def body(
        role_ref, len_ref, q_ref, k_hbm, v_hbm, nk_ref, nv_ref, w_hbm,
        theirs_ref, mine_ref, k_ref, v_ref, w_ref, attn_ref, k_sem, v_sem, w_sem,
    ):
        def copy(hbm, ref, sem, i):
            place = pl.ds(i * step, step)
            return pltpu.make_async_copy(hbm.at[place], ref.at[place], sem.at[i])

        weights = []
        for s in range(2):
            side = role_ref[0] if s else 1 - role_ref[0]
            start = pl.multiple_of(side * half, half)
            for i in range(4):
                place = pl.ds(i * (depth // 4), depth // 4)
                weights.append(
                    pltpu.make_async_copy(
                        w_hbm.at[place, pl.ds(start, half)],
                        w_ref.at[s, place],
                        w_sem.at[4 * s + i],
                    )
                )
        for i in range(blocks):
            copy(k_hbm, k_ref, k_sem, i).start()
            copy(v_hbm, v_ref, v_sem, i).start()
        for i in range(blocks):
            place = slice(i * step, (i + 1) * step)
            q = q_ref[place].reshape(step, group, size)
            copy(k_hbm, k_ref, k_sem, i).wait()
            if i == 0:
                for weight in weights:
                    weight.start()
            scores = lax.dot_general(
                q, k_ref[place], (((2,), (2,)), ((0,), (0,))), preferred_element_type=F32
            )
            scores = scores * scale
            fresh = jnp.sum(
                q.astype(F32) * nk_ref[place].astype(F32)[:, None, :], axis=2, keepdims=True
            )
            fresh = fresh * scale
            position = lax.broadcasted_iota(jnp.int32, (step, group, cache), 2)
            row = lax.broadcasted_iota(jnp.int32, (step, group, cache), 0)
            limit = jnp.full((step, group, cache), len_ref[i * step])
            for j in range(1, step):
                limit = jnp.where(row == j, len_ref[i * step + j], limit)
            scores = jnp.where(position < limit, scores, -jnp.inf)
            top = jnp.maximum(jnp.max(scores, axis=2, keepdims=True), fresh)
            expo = jnp.exp(scores - top)
            expo_new = jnp.exp(fresh - top)
            inverse = 1.0 / (jnp.sum(expo, axis=2, keepdims=True) + expo_new)
            probs = (expo * inverse).astype(BF)
            probs_new = (expo_new * inverse).astype(BF).astype(F32)
            copy(v_hbm, v_ref, v_sem, i).wait()
            result = lax.dot_general(
                probs, v_ref[place], (((2,), (1,)), ((0,), (0,))), preferred_element_type=F32
            )
            result = result + probs_new * nv_ref[place].astype(F32)[:, None, :]
            attn_ref[place, :] = result.reshape(step, depth).astype(BF)
        for weight in weights[:4]:
            weight.wait()
        product = jnp.dot(attn_ref[...], w_ref[0], preferred_element_type=F32)
        theirs_ref[...] = product.astype(BF)
        for weight in weights[4:]:
            weight.wait()
        mine_ref[...] = jnp.dot(attn_ref[...], w_ref[1], preferred_element_type=F32)

    return pl.pallas_call(
        body,
        out_shape=[
            jax.ShapeDtypeStruct((rows, half), BF),
            jax.ShapeDtypeStruct((rows, half), F32),
        ],
        in_specs=[
            pl.BlockSpec(memory_space=pltpu.SMEM),
            pl.BlockSpec(memory_space=pltpu.SMEM),
            pl.BlockSpec(memory_space=pltpu.VMEM),
            pl.BlockSpec(memory_space=pltpu.HBM),
            pl.BlockSpec(memory_space=pltpu.HBM),
            pl.BlockSpec(memory_space=pltpu.VMEM),
            pl.BlockSpec(memory_space=pltpu.VMEM),
            pl.BlockSpec(memory_space=pltpu.HBM),
        ],
        out_specs=whole(2),
        scratch_shapes=[
            pltpu.VMEM((rows, cache, size), BF),
            pltpu.VMEM((rows, cache, size), BF),
            pltpu.VMEM((2, depth, half), BF),
            pltpu.VMEM((rows, depth), BF),
            pltpu.SemaphoreType.DMA((blocks,)),
            pltpu.SemaphoreType.DMA((blocks,)),
            pltpu.SemaphoreType.DMA((8,)),
        ],
        compiler_params=pltpu.CompilerParams(vmem_limit_bytes=57 << 20),
        cost_estimate=pl.CostEstimate(
            flops=0, bytes_accessed=1 << 20, transcendentals=0
        ),
        name="attend",
    )(role.reshape(1), lengths, queries, k_cache, value_cache, new_key, new_value, output_weight)


def of_expert(value, e, per_dev, capacity):
    rows, columns = value.shape
    blocks = rows // (per_dev * capacity)
    return value.reshape(blocks, per_dev, capacity, columns)[:, e].reshape(
        blocks * capacity, columns
    )


def of_all(values, capacity):
    rows, columns = values[0].shape
    blocks = rows // capacity
    parts = [v.reshape(blocks, 1, capacity, columns) for v in values]
    return jnp.concatenate(parts, axis=1).reshape(len(values) * rows, columns)


def expert_act(tokens, gain, w_gate, w_up, w_down, place_across, w_down_places, e, before, capacity):
    roles, slots, half = tokens.shape
    per_dev, width, quarter = w_gate.shape
    columns = w_down.shape[2] // w_down_places
    piece = columns // roles
    chunk = 512
    rows = slots // per_dev
    done = e * rows

    def body(place_ref, x_ref, gain_ref, g_hbm, u_hbm, w_hbm, *rest):
        before_ref = rest[0] if e else None
        act_ref, far_ref, g_ref, u_ref, w_ref, sums, w_sems, sems = rest[1 if e else 0 :]
        last = []
        for s in range(roles):
            start = pl.multiple_of(s * half + place_ref[0] * piece, piece)
            last.append(
                pltpu.make_async_copy(
                    w_hbm.at[e, :, pl.ds(start, piece)],
                    w_ref.at[:, pl.ds(s * piece, piece)],
                    w_sems.at[s],
                )
            )
        copies = []
        for k in range(width // chunk):
            place = pl.ds(k * chunk, chunk)
            copies.append(
                [
                    pltpu.make_async_copy(hbm.at[e, place], ref.at[place], sems.at[2 * k + i])
                    for i, (hbm, ref) in enumerate(((g_hbm, g_ref), (u_hbm, u_ref)))
                ]
            )
        for pair in copies:
            for copy in pair:
                copy.start()
        for copy in last:
            copy.start()
        square = jnp.zeros((rows, 1), F32)
        for k in range(width // chunk):
            s, place = divmod(k * chunk, half)
            x = x_ref[s, :, place : place + chunk].astype(F32)
            x = of_expert(x, e, per_dev, capacity)
            plain = x * (1.0 / gain_ref[s, :, place : place + chunk])
            square = square + jnp.sum(plain * plain, axis=1, keepdims=True)
            x = x.astype(BF)
            for copy in copies[k]:
                copy.wait()
            for i, ref in enumerate((g_ref, u_ref)):
                product = jnp.dot(
                    x, ref[k * chunk : (k + 1) * chunk], preferred_element_type=F32
                )
                sums[i] = product + sums[i] if k else product
        inverse = lax.rsqrt(square / width + EPS)
        gate, upper = sums[0] * inverse, sums[1] * inverse
        act = (gate / (1.0 + jnp.exp(-gate)) * upper).astype(BF)
        if e:
            act_ref[:done] = before_ref[...]
        act_ref[done:] = act
        for copy in last:
            copy.wait()
        far_ref[...] = jnp.dot(act, w_ref[...], preferred_element_type=F32).astype(BF)

    return pl.pallas_call(
        body,
        out_shape=[
            jax.ShapeDtypeStruct((done + rows, quarter), BF),
            jax.ShapeDtypeStruct((rows, columns), BF),
        ],
        in_specs=[pl.BlockSpec(memory_space=pltpu.SMEM)]
        + whole(2)
        + [pl.BlockSpec(memory_space=pltpu.HBM)] * 3
        + whole(1 if e else 0),
        out_specs=whole(2),
        scratch_shapes=[
            pltpu.VMEM((width, quarter), BF),
            pltpu.VMEM((width, quarter), BF),
            pltpu.VMEM((quarter, columns), BF),
            pltpu.VMEM((2, rows, quarter), F32),
            pltpu.SemaphoreType.DMA((roles,)),
            pltpu.SemaphoreType.DMA((2 * (width // chunk),)),
        ],
        compiler_params=pltpu.CompilerParams(vmem_limit_bytes=49 << 20),
        cost_estimate=pl.CostEstimate(
            flops=4 * rows * width * quarter, bytes_accessed=6 << 20, transcendentals=0
        ),
        name=f"expert_act_{e}",
    )(place_across.reshape(1), tokens, gain, w_gate, w_up, w_down, *([before] if e else []))


def own_down(act, own, others, fars):
    slots, _ = act.shape
    per_dev = len(own)
    rows = slots // per_dev
    columns = own[0].shape[1]
    count, early = len(others), len(fars)

    def body(a_ref, *refs):
        w_refs, sources = refs[:per_dev], refs[per_dev : per_dev + count]
        far_refs, (out_ref, *targets, sems) = refs[per_dev + count :][:early], refs[per_dev + count + early :]
        copies = [
            pltpu.make_async_copy(source, target, sems.at[i])
            for i, (source, target) in enumerate(zip(sources, targets))
        ]
        for copy in copies:
            copy.start()
        for e in range(per_dev):
            place = slice(e * rows, (e + 1) * rows)
            value = jnp.dot(a_ref[place], w_refs[e][...], preferred_element_type=F32)
            if e < early:
                value = value + far_refs[e][...].astype(F32)
            out_ref[place] = value
        for copy in copies:
            copy.wait()

    return pl.pallas_call(
        body,
        out_shape=[jax.ShapeDtypeStruct((slots, columns), F32)]
        + [jax.ShapeDtypeStruct(w.shape, BF) for w in others],
        in_specs=whole(1 + per_dev)
        + [pl.BlockSpec(memory_space=pltpu.HBM)] * count
        + whole(early),
        out_specs=whole(1 + count),
        scratch_shapes=[pltpu.SemaphoreType.DMA((count,))],
        compiler_params=pltpu.CompilerParams(vmem_limit_bytes=44 << 20),
        cost_estimate=pl.CostEstimate(flops=0, bytes_accessed=8 << 20, transcendentals=0),
        name="own_down",
    )(act, *own, *others, *fars)


def experts_down(acts, downs, own, far, capacity, roles):
    count = len(acts)
    slots, _ = acts[0].shape
    per_dev = len(downs[0])
    rows = slots // per_dev
    columns = far.shape[1]
    piece = columns // roles

    def body(*refs):
        a_refs, w_refs = refs[:count], refs[count:-3]
        own_ref, far_ref, out_ref = refs[-3:]
        for s in range(roles):
            place = slice(s * piece, (s + 1) * piece)
            totals = []
            for e in range(per_dev):
                total = own_ref[e * rows : (e + 1) * rows, place]
                for i in range(count):
                    total = total + jnp.dot(
                        a_refs[i][e * rows : (e + 1) * rows],
                        w_refs[i * per_dev + e][:, place],
                        preferred_element_type=F32,
                    )
                if e == per_dev - 1:
                    total = total + far_ref[:, place].astype(F32)
                totals.append(total)
            out_ref[s * slots : (s + 1) * slots] = of_all(totals, capacity).astype(BF)

    flat = [w for each in downs for w in each]
    return pl.pallas_call(
        body,
        out_shape=jax.ShapeDtypeStruct((roles * slots, piece), BF),
        in_specs=whole(count + len(flat) + 2),
        out_specs=pl.BlockSpec(memory_space=pltpu.VMEM),
        compiler_params=pltpu.CompilerParams(vmem_limit_bytes=24 << 20),
        name="experts_down",
    )(*acts, *flat, own, far)


def per_device(
    queries,
    k_cache,
    value_cache,
    new_token_key,
    new_token_value,
    lengths,
    output_weight,
    residual,
    norm_gain,
    routes,
    route_scores,
    w_gate,
    w_up,
    w_down,
):
    rows_here = queries.shape[0]
    width = residual.shape[1]
    roles = lax.axis_size("role")
    heads_count = lax.axis_size("heads")
    shards = lax.axis_size("rows")
    half = width // roles
    piece = half // heads_count
    per_dev, _, quarter = w_gate.shape
    experts = per_dev * shards * roles
    capacity = 8
    role = lax.axis_index("role")
    head = lax.axis_index("heads")
    swap = [(i, roles - 1 - i) for i in range(roles)]

    def shift(x, step):
        return lax.ppermute(
            x, "heads", [(i, (i + step) % heads_count) for i in range(heads_count)]
        )

    theirs, mine = attend(
        queries[:, 0, 0],
        k_cache[:, 0],
        value_cache[:, 0],
        new_token_key[:, 0],
        new_token_value[:, 0],
        lengths,
        output_weight[0, 0],
        role,
    )
    received = lax.ppermute(theirs, "role", swap)
    chip = (mine + received.astype(F32)).astype(BF)
    chip, w_down = lax.optimization_barrier((chip, w_down))
    across, near = heads_count // 2, (0, 1, heads_count - 1)
    pieces = [(step, e) for step in near for e in range(per_dev)]
    rest = cut_down(w_down, head, heads_count, roles, pieces)
    total = chip.astype(F32)
    for step in range(1, heads_count):
        total = total + shift(chip, step).astype(F32)
    first = role == 0
    resid = jnp.where(first, residual[:, :half], residual[:, half:]).astype(F32)
    gain = jnp.where(first, norm_gain[:half], norm_gain[half:])
    hidden = resid + total
    hidden, *rest = lax.optimization_barrier((hidden, *rest))
    downs = [
        [shift(part, step) if step else part for part in rest[i * per_dev : (i + 1) * per_dev]]
        for i, step in enumerate(near)
    ]
    scaled = (hidden * gain).astype(BF)

    named = routes[:, :, None] == jnp.arange(experts, dtype=jnp.int32)
    chosen = jnp.any(named, axis=1)
    shares = route_scores / jnp.sum(route_scores, axis=1, keepdims=True)
    coef = jnp.sum(jnp.where(named, shares[:, :, None], F32(0.0)), axis=1)
    order = jnp.arange(rows_here, dtype=jnp.int32)
    before = (order[None, :] < order[:, None]).astype(BF)
    rank = jnp.dot(before, chosen.astype(BF), preferred_element_type=F32).astype(jnp.int32)
    taken = chosen[:, :, None] & (rank[:, :, None] == jnp.arange(capacity, dtype=jnp.int32))
    slots = experts * capacity
    pick = taken.reshape(rows_here, slots).astype(BF)
    mixing = jnp.where(taken, coef[:, :, None], F32(0.0)).reshape(rows_here, slots)

    outgoing = lax.dot_general(
        pick, scaled, (((0,), (0,)), ((), ())), preferred_element_type=F32
    ).astype(BF)
    outgoing = outgoing.reshape(roles * shards, per_dev * capacity, half)
    incoming = lax.all_to_all(outgoing, ("role", "rows"), 0, 0, tiled=True)
    tokens = incoming.reshape(roles, shards * per_dev * capacity, half)
    flat_gain = norm_gain.reshape(roles, 1, half)
    opposite = lax.rem(head + across, heads_count)
    act, fars = None, []
    for e in range(per_dev):
        act, far = expert_act(
            tokens, flat_gain, w_gate, w_up, w_down, opposite, heads_count, e, act, capacity
        )
        fars.append(shift(far, across))
    acts = [shift(act, step) for step in near[1:]]
    others = [w for each in downs[1:] for w in each]
    act, *others = lax.optimization_barrier((act, *others))
    own, *others = own_down(act, downs[0], others, fars[:-1])
    others = [others[i : i + per_dev] for i in range(0, len(others), per_dev)]
    result = experts_down(acts, others, own, fars[-1], capacity, roles)
    result = result.reshape(roles * shards, per_dev * capacity, piece)
    returned = lax.all_to_all(result, ("role", "rows"), 0, 0, tiled=True)
    returned = returned.reshape(slots, piece)
    mix_high = mixing.astype(BF)
    mix_low = (mixing - mix_high.astype(F32)).astype(BF)
    moe = jnp.dot(mix_high, returned, preferred_element_type=F32) + jnp.dot(
        mix_low, returned, preferred_element_type=F32
    )
    own = lax.dynamic_slice_in_dim(hidden, head * piece, piece, 1)
    return (own + moe).astype(BF)


def solution(mesh):
    in_specs = (
        P("rows", "role", "heads", None),
        P("rows", "heads", None, None),
        P("rows", "heads", None, None),
        P("rows", "heads", None),
        P("rows", "heads", None),
        P("rows"),
        P("role", "heads", None, None),
        P("rows", None),
        P(),
        P("rows", None),
        P("rows", None),
        P(("role", "rows"), None, "heads"),
        P(("role", "rows"), None, "heads"),
        P(("role", "rows"), "heads", None),
    )
    out_specs = P("rows", ("role", "heads"))
    return jax.shard_map(
        per_device, mesh=mesh, in_specs=in_specs, out_specs=out_specs, check_vma=False
    )
```
